32 devices in a mesh: expert: 8 (over z, x), shard: 4 (over y, core).
Axes of the slice: x: 2, y: 2, z: 4, core: 2. Of those that a mesh axis runs over, the one named last changes fastest.
Arguments:
- tokens: bfloat16 [192, 197, 768], P(('expert', 'shard')), may hold values from -6 to 6
- ln1_gain: bfloat16 [768], P('shard'), may hold values from 0.5 to 1.5
- ln1_bias: bfloat16 [768], P('shard'), may hold values from -1.796875 to 1.796875
- qkv_weight: bfloat16 [768, 2304], P('shard'), may hold values from -0.3125 to 0.3125
- out_weight: bfloat16 [768, 768], P('shard'), may hold values from -1.25 to 1.25
- ln2_gain: bfloat16 [768], P('shard'), may hold values from 0.5 to 1.5
- ln2_bias: bfloat16 [768], P('shard'), may hold values from -1.796875 to 1.796875
- router_weight: bfloat16 [768, 8], P('shard'), may hold values from -0.15625 to 0.15625
- up_weight: bfloat16 [3072, 8, 768], P('shard', 'expert'), may hold values from -0.21875 to 0.21875
- down_weight: bfloat16 [3072, 8, 768], P('shard', 'expert'), may hold values from -0.4375 to 0.4375
- routes: int32 [192, 197, 2], P(('expert', 'shard')), may hold values from 0 to 7, as said below
- slots: int32 [192, 197, 2], P(('expert', 'shard')), may hold values from 0 to 368, as said below
- keep: int32 [192, 197, 2], P(('expert', 'shard')), may hold values from 0 to 1, as said below
- cotangent: bfloat16 [192, 197, 768], P(('expert', 'shard')), may hold values from -6 to 6
Outputs:
- block_out: bfloat16 [192, 197, 768], P(('expert', 'shard'))
- tokens_grad: bfloat16 [192, 197, 768], P(('expert', 'shard'))
- ln1_gain_grad: float32 [768], P('shard')
- ln1_bias_grad: float32 [768], P('shard')
- qkv_grad: float32 [768, 2304], P('shard')
- out_grad: float32 [768, 768], P('shard')
- ln2_gain_grad: float32 [768], P('shard')
- ln2_bias_grad: float32 [768], P('shard')
- router_grad: float32 [768, 8], P('shard')
- up_grad: float32 [3072, 8, 768], P('shard', 'expert')
- down_grad: float32 [3072, 8, 768], P('shard', 'expert')
The draws below stay inside these ranges and needn't reach their ends.
Inputs may be any that keep to these rules, and one draw needn't show every extreme that they name: `routes`: each token names two different experts. Of the assignments (in order of token, then choice) that the tokens of one device make to one expert, the first 369 have keep 1 and slots 0, 1, 2, ... in that order; the later ones have keep 0 and slot 368. In every draw some expert receives 369 kept assignments from every device. `keep`: 1 exactly for the kept assignments described for slots.
All inputs are finite; a program needn't handle non-finite values.
Results may differ from the reference program's by a relative error of at most 0.014.
Values may be sent and summed in bfloat16 or wider, within the bound.
No kernel may reach another device: no remote copies, remote signals or barrier semaphores. Data moves between devices by JAX's collectives and lax.ppermute only.
A program may use at most 320 MiB of HBM per device.

```python
import jax
import jax.numpy as jnp
from jax import lax

D = 768
HEADS = 12
HEAD_DIM = 64
FF = 3072
SEQ = 197
IMG_DEV = 6
EXPERTS = 8
IMAGES = 192
TOK_DEV = 1182
CAP = 369


def route_table(key):
    blocks = IMAGES // IMG_DEV
    per_block = IMG_DEV * SEQ
    keys = jax.random.split(key, 4)
    hot = jax.random.randint(keys[0], (), 0, EXPERTS)
    ranks = jax.vmap(lambda sub: jax.random.permutation(sub, per_block))(jax.random.split(keys[1], blocks))
    busy = min(per_block, CAP + per_block // 8)
    other = jax.random.randint(keys[2], (blocks, per_block), 0, EXPERTS - 1)
    other = other + (other >= hot).astype(jnp.int32)
    first = jnp.where(ranks < busy, hot, other)
    second = (first + jax.random.randint(keys[3], (blocks, per_block), 1, EXPERTS)) % EXPERTS
    picks = jnp.stack([first, second], -1).reshape(blocks, 2 * per_block).astype(jnp.int32)
    hits = (picks[:, :, None] == jnp.arange(EXPERTS, dtype=jnp.int32)[None, None, :]).astype(jnp.int32)
    order = jnp.cumsum(hits, 1) - 1
    place = jnp.sum(order * hits, -1)
    kept = (place < CAP).astype(jnp.int32)
    place = jnp.where(kept > 0, place, CAP - 1)
    shape = (IMAGES, SEQ, 2)
    return (picks.reshape(shape).astype(jnp.int32), place.reshape(shape).astype(jnp.int32), kept.reshape(shape))


def draw_routes(key, part):
    table = route_table(key)
    return table[0]


def draw_slots(key, part):
    table = route_table(key)
    return table[1]


def draw_keep(key, part):
    table = route_table(key)
    return table[2]


def steps_of(stream_key, extent, cuts, low, high):
    level = 1.0
    for axis_at, parts in cuts:
        draws = jax.random.uniform(jax.random.fold_in(jax.random.fold_in(stream_key, 6), axis_at), (parts,), jnp.float32, low / len(cuts), high / len(cuts))
        level = level * jnp.repeat(jnp.exp(draws), extent[axis_at] // parts).reshape((-1,) + (1,) * (len(extent) - 1 - axis_at))
    return level


def normal_values(own_key, extent, scale, limit, cuts=(), kind=jnp.bfloat16):
    array = scale * jax.random.normal(own_key, extent, jnp.float32)
    if cuts:
        array = array * steps_of(own_key, extent, cuts, -0.22, 0.18)
    return jnp.clip(array, -limit, limit).astype(kind)


def setup_inputs(seed: int = 0) -> dict:
    seeds = jax.random.split(jax.random.key(seed), 15)
    tokens = normal_values(seeds[0], (IMAGES, SEQ, D), 1.0, 6.0, ((0, 32),))
    ln1_gain = jnp.clip(1.0 + 0.1 * jax.random.normal(seeds[1], (D,), jnp.float32), 0.5, 1.5).astype(jnp.bfloat16)
    ln1_bias = normal_values(seeds[2], (D,), 0.3, 1.796875, ((0, 4),))
    qkv_weight = normal_values(seeds[3], (D, 3 * D), (D // 2) ** -0.5, 0.3125, ((0, 4),))
    out_weight = normal_values(seeds[4], (D, D), (D // 32) ** -0.5, 1.25, ((0, 4),))
    ln2_gain = jnp.clip(1.0 + 0.1 * jax.random.normal(seeds[5], (D,), jnp.float32), 0.5, 1.5).astype(jnp.bfloat16)
    ln2_bias = normal_values(seeds[6], (D,), 0.3, 1.796875, ((0, 4),))
    router_weight = normal_values(seeds[7], (D, EXPERTS), (2 * D) ** -0.5, 0.15625, ((0, 4),))
    up_weight = normal_values(seeds[8], (FF, EXPERTS, D), D ** -0.5, 0.21875, ((0, 4), (1, 8)))
    down_weight = normal_values(seeds[9], (FF, EXPERTS, D), (max(1, FF * 4 // (EXPERTS * EXPERTS))) ** -0.5, 0.4375, ((0, 4), (1, 8)))
    routes = draw_routes(jax.random.fold_in(seeds[14], 71), 0)
    slots = draw_slots(jax.random.fold_in(seeds[14], 71), 0)
    keep = draw_keep(jax.random.fold_in(seeds[14], 71), 0)
    cotangent = normal_values(seeds[13], (IMAGES, SEQ, D), 1.0, 6.0, ((0, 32),))
    return dict(tokens=tokens, ln1_gain=ln1_gain, ln1_bias=ln1_bias, qkv_weight=qkv_weight, out_weight=out_weight, ln2_gain=ln2_gain, ln2_bias=ln2_bias, router_weight=router_weight, up_weight=up_weight, down_weight=down_weight, routes=routes, slots=slots, keep=keep, cotangent=cotangent)


EPSILON = 1e-06
HIGH = lax.Precision.HIGHEST

@jax.custom_vjp
def low(v):
    return lax.optimization_barrier(v.astype(jnp.bfloat16)).astype(jnp.float32)

@jax.custom_vjp
def low_back(v):
    return v

def low_keep(v):
    return (low(v), None)

def low_pass(kept, grad):
    return (grad,)

def back_keep(v):
    return (v, None)

def back_low(kept, grad):
    return (low(grad),)
low.defvjp(low_keep, low_pass)
low_back.defvjp(back_keep, back_low)

def layer_norm(value, gain, shift):
    mean = lax.optimization_barrier(jnp.mean(value, -1, keepdims=True))
    centered = value - mean
    spread = lax.optimization_barrier(jnp.mean(centered * centered, -1, keepdims=True))
    return centered * lax.rsqrt(spread + EPSILON) * gain + shift

def attend(block, gain1, bias1, w_qkv, w_out):
    count = block.shape[0]
    normed = low(layer_norm(block, gain1, bias1))
    qkv = low(low_back(jnp.einsum('gsd,de->gse', normed, w_qkv, precision=HIGH)))
    split = qkv.reshape(count, SEQ, 3, HEADS, HEAD_DIM)
    query, keys, values = (split[:, :, 0], split[:, :, 1], split[:, :, 2])
    scores = low_back(jnp.einsum('gqhc,gkhc->ghqk', query, keys, precision=HIGH) * HEAD_DIM ** (-0.5))
    probs = low(jax.nn.softmax(scores, -1))
    mixed = jnp.einsum('ghqk,gkhc->gqhc', probs, values, precision=HIGH).reshape(count, SEQ, D)
    mixed = low(low_back(mixed))
    return block + low_back(jnp.einsum('gsd,de->gse', mixed, w_out, precision=HIGH))

def expert(rows, w_up, w_down):
    before = low_back(jnp.dot(rows, w_up.T, precision=HIGH))
    active = low(jax.nn.gelu(before))
    return low(low_back(jnp.dot(active, w_down, precision=HIGH)))

def forward(tokens, gain1, bias1, w_qkv, w_out, gain2, bias2, w_router, w_up, w_down, routes, slots, keep):
    groups = tokens.reshape(IMAGES // IMG_DEV, IMG_DEV, SEQ, D)

    def attend_group(block):
        return attend(block, gain1, bias1, w_qkv, w_out)
    attended = lax.map(jax.checkpoint(attend_group), groups).reshape(IMAGES * SEQ, D)
    normed = low(layer_norm(attended, gain2, bias2))
    logits = jnp.dot(normed, w_router, precision=HIGH)
    probs = jax.nn.softmax(logits, -1)
    route_rows = routes.reshape(-1, 2).astype(jnp.int32)
    kept = keep.reshape(-1, 2).astype(jnp.float32)
    gates = jnp.take_along_axis(probs, route_rows, 1) * kept
    total_rows = IMAGES * SEQ
    blocks = IMAGES // IMG_DEV
    spread = blocks * CAP
    block_of = (jnp.arange(total_rows, dtype=jnp.int32) // TOK_DEV)[:, None]
    position = route_rows * spread + block_of * CAP + slots.reshape(-1, 2).astype(jnp.int32)
    position = jnp.where(kept > 0, position, EXPERTS * spread).reshape(-1).astype(jnp.int32)
    filled = jnp.zeros((EXPERTS * spread + 1, D), jnp.float32).at[position].add(jnp.repeat(normed, 2, axis=0))
    arrived = low_back(filled[:EXPERTS * spread]).reshape(EXPERTS, spread, D)

    def run_expert(items):
        return expert(items[0], items[1], items[2])
    produced = lax.map(jax.checkpoint(run_expert), (arrived, jnp.moveaxis(w_up, 1, 0), jnp.moveaxis(w_down, 1, 0)))
    padded = jnp.concatenate([produced.reshape(EXPERTS * spread, D), jnp.zeros((1, D), jnp.float32)], 0)
    picked = padded[position].reshape(total_rows, 2, D)
    return attended + lax.optimization_barrier(jnp.sum(gates[:, :, None] * picked, 1))

def reference(tokens, ln1_gain, ln1_bias, qkv_weight, out_weight, ln2_gain, ln2_bias, router_weight, up_weight, down_weight, routes, slots, keep, cotangent):
    floats = [value.astype(jnp.float32) for value in (tokens, ln1_gain, ln1_bias, qkv_weight, out_weight, ln2_gain, ln2_bias, router_weight, up_weight, down_weight)]

    def run(tok, gain1, bias1, w_qkv, w_out, gain2, bias2, w_router, w_up, w_down):
        return forward(tok, gain1, bias1, w_qkv, w_out, gain2, bias2, w_router, w_up, w_down, routes, slots, keep)
    output, pullback = jax.vjp(run, *floats)
    grads = pullback(cotangent.reshape(IMAGES * SEQ, D).astype(jnp.float32))
    return (output.astype(jnp.bfloat16).reshape(IMAGES, SEQ, D), grads[0].astype(jnp.bfloat16).reshape(IMAGES, SEQ, D), grads[1], grads[2], grads[3], grads[4], grads[5], grads[6], grads[7], grads[8], grads[9])
```

```python
import functools

import jax
import jax.numpy as jnp
from jax import lax
from jax.experimental import pallas as pl
from jax.experimental.pallas import tpu as pltpu
from jax.sharding import PartitionSpec as P

HEADS = 12
EPSILON = 1e-06
CHUNKS = 2
LANES = 128
MIB = 1024 * 1024
BF16 = jnp.bfloat16
F32 = jnp.float32
NN = (((1,), (0,)), ((), ()))
NT = (((1,), (1,)), ((), ()))
TN = (((0,), (0,)), ((), ()))


def dot(a, b, dims=NN):
    return lax.dot_general(a, b, dims, preferred_element_type=F32)


def whole(shape):
    return pl.BlockSpec(shape, lambda *_: (0,) * len(shape), pipeline_mode=pl.Buffered(1))


def call(kernel, grid, in_specs, out_specs, out_shape, scratch, limit):
    return pl.pallas_call(
        kernel,
        grid=grid,
        in_specs=in_specs,
        out_specs=out_specs,
        out_shape=out_shape,
        scratch_shapes=scratch,
        compiler_params=pltpu.CompilerParams(
            vmem_limit_bytes=limit * MIB,
            dimension_semantics=("arbitrary",) * len(grid),
        ),
    )


def normal(value):
    centered = value - jnp.mean(value, -1, keepdims=True)
    inverse = lax.rsqrt(jnp.mean(centered * centered, -1, keepdims=True) + EPSILON)
    return centered * inverse, inverse


def norm_back(grad, gain, unit, inverse):
    scaled = grad * gain
    return inverse * (
        scaled
        - jnp.mean(scaled, -1, keepdims=True)
        - unit * jnp.mean(scaled * unit, -1, keepdims=True)
    )


def one_hot(equal):
    return jnp.where(equal, 1.0, 0.0).astype(BF16)


def padded_rows(source, buffer):
    length = source.shape[1]
    buffer[...] = jnp.zeros_like(buffer)
    buffer[0:length, :] = source[0].astype(buffer.dtype)
    return buffer[...]


def send_images_kernel(codes_ref, source_ref, out_ref, rows):
    images, length, _ = source_ref.shape
    padded = rows.shape[0] // images
    step = pl.program_id(0)

    @pl.when(step == 0)
    def _():
        rows[...] = jnp.zeros_like(rows)
        for image in range(images):
            rows[image * padded : image * padded + length, :] = source_ref[image].astype(F32)

    pick_rows(codes_ref, rows[...].astype(BF16), out_ref, step)


def send_rows_kernel(codes_ref, source_ref, out_ref):
    pick_rows(codes_ref, source_ref[...], out_ref, pl.program_id(0))


def pick_rows(codes_ref, rows, out_ref, step):
    count = out_ref.shape[1]
    tokens = rows.shape[0]
    slot = lax.broadcasted_iota(jnp.int32, (count, tokens), 0) + step * count
    hot = one_hot((slot == codes_ref[0:1, :]) | (slot == codes_ref[1:2, :]))
    out_ref[0] = dot(hot, rows).astype(BF16)


def send(source, codes, experts, count, width):
    tokens = codes.shape[1]
    if source.ndim == 3:
        kernel, scratch = send_images_kernel, [pltpu.VMEM((tokens, width), F32)]
    else:
        kernel, scratch = send_rows_kernel, []
    return call(
        kernel,
        (experts,),
        [whole(codes.shape), whole(source.shape)],
        pl.BlockSpec((1, count, width), lambda e: (e, 0, 0)),
        jax.ShapeDtypeStruct((experts, count, width), BF16),
        scratch,
        40,
    )(codes, source)


def gather_rows(codes, arrays):
    total = None
    for chunk, array in enumerate(arrays):
        slot = lax.broadcasted_iota(jnp.int32, (codes.shape[0], array.shape[0]), 1)
        first = codes[:, 2 * chunk : 2 * chunk + 1]
        second = codes[:, 2 * chunk + 1 : 2 * chunk + 2]
        part = dot(one_hot((slot == first) | (slot == second)), array[...])
        total = part if total is None else total + part
    return total


def attend_kernel(
    tokens_ref, qkv_weight_ref, out_weight_ref, vector_ref,
    qkv_ref, mixed_ref, attended_ref, first_ref, second_ref, buffer,
):
    length = tokens_ref.shape[1]
    padded, width = buffer.shape
    value = padded_rows(tokens_ref, buffer)
    unit, _ = normal(value)
    first = (unit * vector_ref[0:1, :] + vector_ref[1:2, :]).astype(BF16)
    first_ref[0] = first
    qkv_ref[0] = dot(first, qkv_weight_ref[...]).astype(BF16)
    scale = (width // HEADS) ** (-0.5)
    per_tile = LANES * HEADS // width
    lane = lax.broadcasted_iota(jnp.int32, (padded, LANES), 1) // (width // HEADS)
    real = lax.broadcasted_iota(jnp.int32, (padded, padded), 1) < length
    for tile in range(width // LANES):
        at = tile * LANES
        query = qkv_ref[0, :, at : at + LANES]
        keys = qkv_ref[0, :, width + at : width + at + LANES]
        values = qkv_ref[0, :, 2 * width + at : 2 * width + at + LANES]
        result = None
        for head in range(per_tile):
            chosen = jnp.where(lane == head, query.astype(F32) * scale, 0.0).astype(BF16)
            scores = jnp.where(real, dot(chosen, keys, NT), -1e30)
            raised = jnp.exp(scores - jnp.max(scores, -1, keepdims=True))
            probs = raised * (1.0 / jnp.sum(raised, -1, keepdims=True))
            part = dot(probs.astype(BF16), values)
            result = part if result is None else jnp.where(lane == head, part, result)
        mixed_ref[0, :, at : at + LANES] = result.astype(BF16)
    attended = value + dot(mixed_ref[0], out_weight_ref[...])
    attended_ref[0] = attended
    unit, _ = normal(attended)
    second_ref[0] = (unit * vector_ref[2:3, :] + vector_ref[3:4, :]).astype(BF16)


def attend(tokens, weights, vectors, padded):
    images, length, width = tokens.shape
    image = lambda cols: pl.BlockSpec((1, padded, cols), lambda i: (i, 0, 0))
    shape = lambda cols, kind: jax.ShapeDtypeStruct((images, padded, cols), kind)
    return call(
        attend_kernel,
        (images,),
        [
            pl.BlockSpec((1, length, width), lambda i: (i, 0, 0)),
            pl.BlockSpec((width, 3 * width), lambda i: (0, 0), pipeline_mode=pl.Buffered(1)),
            pl.BlockSpec((width, width), lambda i: (0, 3), pipeline_mode=pl.Buffered(1)),
            whole(vectors.shape),
        ],
        [image(3 * width), image(width), image(width), image(width), image(width)],
        [
            shape(3 * width, BF16), shape(width, BF16), shape(width, F32),
            shape(width, BF16), shape(width, BF16),
        ],
        [pltpu.VMEM((padded, width), F32)],
        40,
    )(tokens, weights, weights, vectors)


def gelu_pair(value):
    root = 0.7978845608028654
    cubic = 0.044715
    square = value * value
    bent = jnp.tanh(root * value * (1.0 + cubic * square))
    half = 0.5 * (1.0 + bent)
    slope = half + 0.5 * value * (1.0 - bent * bent) * (root * (1.0 + 3.0 * cubic * square))
    return value * half, slope


def expert_kernel(
    experts, block,
    mine_ref, x_ref, g_ref, up_ref, down_ref, router_ref,
    active_ref, before_ref, scaled_ref, out_ref, back_ref, logit_ref,
    out_sum, back_sum, probs_ref,
):
    step = pl.program_id(0)
    blocks = x_ref.shape[0] // block
    mine = mine_ref[0:1, :]

    def rows_of(index):
        return pl.ds(pl.multiple_of(index * block, block), block)

    @pl.when(step == 0)
    def _():
        def start(index, _):
            rows = rows_of(index)
            logits = dot(x_ref[rows, :], router_ref[...])
            column = lax.broadcasted_iota(jnp.int32, logits.shape, 1)
            logits = jnp.where(column < experts, logits, -1e30)
            raised = jnp.exp(logits - jnp.max(logits, -1, keepdims=True))
            probs = raised / jnp.sum(raised, -1, keepdims=True)
            probs_ref[rows, :] = probs
            gate = jnp.sum(probs * mine, -1, keepdims=True)
            scaled_ref[rows, :] = (gate * g_ref[rows, :].astype(F32)).astype(BF16)
            out_sum[rows, :] = jnp.zeros((block, out_sum.shape[1]), F32)
            back_sum[rows, :] = jnp.zeros((block, back_sum.shape[1]), F32)
            return 0

        lax.fori_loop(0, blocks, start, 0)

    def work(index, _):
        rows = rows_of(index)
        before = dot(x_ref[rows, :], up_ref[...], NT)
        active_grad = dot(scaled_ref[rows, :], down_ref[...], NT)
        active, slope = gelu_pair(before)
        active = active.astype(BF16)
        before_grad = (active_grad * slope).astype(BF16)
        active_ref[rows, :] = active
        before_ref[rows, :] = before_grad
        out_sum[rows, :] += dot(active, down_ref[...])
        back_sum[rows, :] += dot(before_grad, up_ref[...])
        return 0

    lax.fori_loop(0, blocks, work, 0)

    @pl.when(step == pl.num_programs(0) - 1)
    def _():
        def finish(index, _):
            rows = rows_of(index)
            made = out_sum[rows, :].astype(BF16).astype(F32)
            probs = probs_ref[rows, :]
            gate = jnp.sum(probs * mine, -1, keepdims=True)
            gate_grad = jnp.sum(made * g_ref[rows, :].astype(F32), -1, keepdims=True)
            logit = (gate_grad * gate * (mine - probs)).astype(BF16)
            logit_ref[rows, :] = logit
            out_ref[rows, :] = (gate * made).astype(BF16)
            back_ref[rows, :] = (back_sum[rows, :] + dot(logit, router_ref[...], NT)).astype(BF16)
            return 0

        lax.fori_loop(0, blocks, finish, 0)


def run_expert(mine, x, g, up, down, weights, experts):
    rows, width = x.shape
    hidden = up.shape[0]
    part = 512
    block = 256
    last = weights.shape[1] // LANES - 1
    wide = pl.BlockSpec((rows, part), lambda f: (0, f))
    weight = pl.BlockSpec((part, width), lambda f: (f, 0))
    return call(
        functools.partial(expert_kernel, experts, block),
        (hidden // part,),
        [
            whole(mine.shape), whole(x.shape), whole(g.shape), weight, weight,
            pl.BlockSpec((width, LANES), lambda f: (0, last), pipeline_mode=pl.Buffered(1)),
        ],
        [wide, wide, whole((rows, width)), whole((rows, width)), whole((rows, width)), whole((rows, LANES))],
        [
            jax.ShapeDtypeStruct((rows, hidden), BF16), jax.ShapeDtypeStruct((rows, hidden), BF16),
            jax.ShapeDtypeStruct((rows, width), BF16), jax.ShapeDtypeStruct((rows, width), BF16),
            jax.ShapeDtypeStruct((rows, width), BF16), jax.ShapeDtypeStruct((rows, LANES), BF16),
        ],
        [pltpu.VMEM((rows, width), F32), pltpu.VMEM((rows, width), F32), pltpu.VMEM((rows, LANES), F32)],
        52,
    )(mine, x, g, up, down, weights)


def attend_back_kernel(*refs):
    codes_ref, *refs = refs
    returned, refs = refs[:CHUNKS], refs[CHUNKS:]
    (
        cotangent_ref, tokens_ref, attended_ref, qkv_ref,
        qkv_weight_ref, out_weight_ref, vector_ref,
        tokens_grad_ref, branch_ref, rows_grad_ref, sums_ref, buffer,
    ) = refs
    length = tokens_ref.shape[1]
    padded, width = buffer.shape

    @pl.when(pl.program_id(0) == 0)
    def _():
        sums_ref[...] = jnp.zeros_like(sums_ref)

    second_grad = gather_rows(codes_ref[0], returned)
    unit, inverse = normal(attended_ref[0])
    sums_ref[2:3, :] += jnp.sum(second_grad * unit, 0, keepdims=True)
    sums_ref[3:4, :] += jnp.sum(second_grad, 0, keepdims=True)
    attended_grad = padded_rows(cotangent_ref, buffer) + norm_back(
        second_grad, vector_ref[2:3, :], unit, inverse
    )
    branch = attended_grad.astype(BF16)
    branch_ref[0] = branch
    mixed_grad = dot(branch, out_weight_ref[...], NT).astype(BF16)
    scale = (width // HEADS) ** (-0.5)
    per_tile = LANES * HEADS // width
    lane = lax.broadcasted_iota(jnp.int32, (padded, LANES), 1) // (width // HEADS)
    real = lax.broadcasted_iota(jnp.int32, (padded, padded), 0) < length
    for tile in range(width // LANES):
        at = tile * LANES
        query = qkv_ref[0, :, at : at + LANES].astype(F32) * scale
        keys = qkv_ref[0, :, width + at : width + at + LANES]
        values = qkv_ref[0, :, 2 * width + at : 2 * width + at + LANES]
        keys_scaled = keys.astype(F32) * scale
        result = mixed_grad[:, at : at + LANES].astype(F32)
        grads = [None, None, None]
        for head in range(per_tile):
            own = lane == head
            own_query = jnp.where(own, query, 0.0).astype(BF16)
            own_keys = jnp.where(own, keys_scaled, 0.0).astype(BF16)
            own_result = jnp.where(own, result, 0.0).astype(BF16)
            scores = jnp.where(real, dot(keys, own_query, NT), -1e30)
            raised = jnp.exp(scores - jnp.max(scores, 0, keepdims=True))
            probs = raised * (1.0 / jnp.sum(raised, 0, keepdims=True))
            prob_grad = dot(values, own_result, NT)
            score_grad = (
                probs * (prob_grad - jnp.sum(probs * prob_grad, 0, keepdims=True))
            ).astype(BF16)
            parts = (
                dot(score_grad, own_keys, TN),
                dot(score_grad, own_query),
                dot(probs.astype(BF16), own_result),
            )
            grads = [part if old is None else old + part for old, part in zip(grads, parts)]
        for index, grad in enumerate(grads):
            start = index * width + at
            rows_grad_ref[0, :, start : start + LANES] = grad.astype(BF16)
    first_grad = dot(rows_grad_ref[0], qkv_weight_ref[...], NT)
    unit, inverse = normal(padded_rows(tokens_ref, buffer))
    sums_ref[0:1, :] += jnp.sum(first_grad * unit, 0, keepdims=True)
    sums_ref[1:2, :] += jnp.sum(first_grad, 0, keepdims=True)
    tokens_grad = attended_grad + norm_back(first_grad, vector_ref[0:1, :], unit, inverse)
    tokens_grad_ref[0] = tokens_grad[0:length, :].astype(BF16)


def attend_back(codes, returned, cotangent, tokens, attended, qkv, weights, vectors):
    images, length, width = tokens.shape
    padded = attended.shape[1]
    image = lambda rows, cols: pl.BlockSpec((1, rows, cols), lambda i: (i, 0, 0))
    return call(
        attend_back_kernel,
        (images,),
        [image(padded, codes.shape[2])]
        + [whole(array.shape) for array in returned]
        + [
            image(length, width), image(length, width), image(padded, width), image(padded, 3 * width),
            pl.BlockSpec((width, 3 * width), lambda i: (0, 0), pipeline_mode=pl.Buffered(1)),
            pl.BlockSpec((width, width), lambda i: (0, 3), pipeline_mode=pl.Buffered(1)),
            whole(vectors.shape),
        ],
        [image(length, width), image(padded, width), image(padded, 3 * width), whole((8, width))],
        [
            jax.ShapeDtypeStruct((images, length, width), BF16),
            jax.ShapeDtypeStruct((images, padded, width), BF16),
            jax.ShapeDtypeStruct((images, padded, 3 * width), BF16),
            jax.ShapeDtypeStruct((8, width), F32),
        ],
        [pltpu.VMEM((padded, width), F32)],
        48,
    )(codes, *returned, cotangent, tokens, attended, qkv, weights, weights, vectors)


def combine_kernel(codes_ref, *refs):
    returned, (attended_ref, out_ref) = refs[:CHUNKS], refs[CHUNKS:]
    total = attended_ref[0] + gather_rows(codes_ref[0], returned)
    out_ref[0] = total[0 : out_ref.shape[1], :].astype(BF16)


def combine(codes, returned, attended, length):
    images, padded, width = attended.shape
    image = lambda rows, cols: pl.BlockSpec((1, rows, cols), lambda i: (i, 0, 0))
    return call(
        combine_kernel,
        (images,),
        [image(padded, codes.shape[2])]
        + [whole(array.shape) for array in returned]
        + [image(padded, width)],
        image(length, width),
        jax.ShapeDtypeStruct((images, length, width), BF16),
        [],
        40,
    )(codes, *returned, attended)


def exchange(array):
    return lax.all_to_all(array, "expert", split_axis=0, concat_axis=0, tiled=True)


def shards(
    tokens,
    ln1_gain,
    ln1_bias,
    qkv_weight,
    out_weight,
    ln2_gain,
    ln2_bias,
    router_weight,
    up_weight,
    down_weight,
    routes,
    slots,
    keep,
    cotangent,
):
    images, length, width = tokens.shape
    rows = images * length
    experts = lax.axis_size("expert")
    assert up_weight.shape[1] == 1 and router_weight.shape[1] == experts
    capacity = max(4, 5 * rows // (2 * experts))
    count = -(-capacity // (16 * CHUNKS)) * 16
    padded = -(-length // 16) * 16

    columns = experts + 4
    spare = -columns % LANES
    small = jnp.concatenate(
        [router_weight, jnp.stack([ln1_gain, ln1_bias, ln2_gain, ln2_bias], 1)], 1
    )
    packed = jnp.concatenate(
        [qkv_weight, out_weight, jnp.pad(small, ((0, 0), (0, spare)))], 1
    )
    weights = lax.all_gather(packed, "shard", axis=0, tiled=True)
    vectors = jnp.pad(
        weights[:, 4 * width + experts : 4 * width + columns].T.astype(F32), ((0, 4), (0, 0))
    )

    chunk_codes = []
    for chunk in range(CHUNKS):
        place = slots - chunk * count
        here = (keep > 0) & (place >= 0) & (place < count)
        chunk_codes.append(jnp.where(here, routes * count + place, -1))
    codes = jnp.pad(
        jnp.concatenate(chunk_codes, -1),
        ((0, 0), (0, padded - length), (0, 0)),
        constant_values=-1,
    )
    flat_codes = codes.reshape(images * padded, 2 * CHUNKS).T
    row_codes = [flat_codes[2 * chunk : 2 * chunk + 2] for chunk in range(CHUNKS)]

    g_sent = [send(cotangent, code, experts, count, width) for code in row_codes]
    g_sent, tokens_in = lax.optimization_barrier((g_sent, tokens))
    g_here = [exchange(array).reshape(experts * count, width) for array in g_sent]

    up = lax.all_gather(up_weight.reshape(-1, width), "shard", axis=0, tiled=True)
    down = lax.all_gather(down_weight.reshape(-1, width), "shard", axis=0, tiled=True)

    qkv, mixed, attended, first, second = attend(tokens_in, weights, vectors, padded)
    flat_second = second.reshape(images * padded, width)
    mine = (
        lax.broadcasted_iota(jnp.int32, (8, LANES), 1) == lax.axis_index("expert")
    ).astype(F32)

    back_here, out_here, wide = [], [], []
    for chunk in range(CHUNKS):
        x = exchange(send(flat_second, row_codes[chunk], experts, count, width))
        x = x.reshape(experts * count, width)
        active, before_grad, scaled, out, back, logit = run_expert(
            mine, x, g_here[chunk], up, down, weights, experts
        )
        wide.append((active, before_grad, scaled, x, logit))
        back_here.append(back.reshape(experts, count, width))
        out_here.append(out.reshape(experts, count, width))

    returned = [exchange(array).reshape(experts * count, width) for array in back_here]
    out_here, returned = lax.optimization_barrier((out_here, returned))
    out_returned = [exchange(array).reshape(experts * count, width) for array in out_here]

    down_full = sum(dot(part[0], part[2], TN) for part in wide)
    up_full = sum(dot(part[1], part[3], TN) for part in wide)
    router_full = sum(dot(part[3], part[4], TN) for part in wide)
    down_grad = lax.psum_scatter(down_full.astype(BF16), "shard", scatter_dimension=0, tiled=True)
    up_grad = lax.psum_scatter(up_full.astype(BF16), "shard", scatter_dimension=0, tiled=True)

    tokens_grad, branch, rows_grad, sums = attend_back(
        codes, returned, cotangent, tokens, attended, qkv, weights, vectors
    )
    flat = lambda array: array.reshape(images * padded, -1)
    qkv_full = dot(flat(first), flat(rows_grad), TN)
    out_full = dot(flat(mixed), flat(branch), TN)
    small_full = jnp.concatenate([router_full[:, :experts], sums[0:4].T], 1)
    layer = jnp.concatenate(
        [qkv_full, out_full, jnp.pad(small_full, ((0, 0), (0, spare)))], 1
    ).astype(BF16)
    layer = lax.psum_scatter(layer, "shard", scatter_dimension=0, tiled=True)
    layer = lax.psum(layer, "expert").astype(F32)
    block_out = combine(codes, out_returned, attended, length)
    tail = 4 * width + experts
    return (
        block_out,
        tokens_grad,
        layer[:, tail],
        layer[:, tail + 1],
        layer[:, : 3 * width],
        layer[:, 3 * width : 4 * width],
        layer[:, tail + 2],
        layer[:, tail + 3],
        layer[:, 4 * width : tail],
        up_grad.astype(F32)[:, None, :],
        down_grad.astype(F32)[:, None, :],
    )


def solution(mesh):
    placed = (
        P(("expert", "shard"), None, None),
        P("shard"),
        P("shard"),
        P("shard", None),
        P("shard", None),
        P("shard"),
        P("shard"),
        P("shard", None),
        P("shard", "expert", None),
        P("shard", "expert", None),
        P(("expert", "shard"), None, None),
        P(("expert", "shard"), None, None),
        P(("expert", "shard"), None, None),
        P(("expert", "shard"), None, None),
    )
    return jax.shard_map(
        shards,
        mesh=mesh,
        in_specs=placed,
        out_specs=(
            P(("expert", "shard"), None, None),
            P(("expert", "shard"), None, None),
            P("shard"),
            P("shard"),
            P("shard", None),
            P("shard", None),
            P("shard"),
            P("shard"),
            P("shard", None),
            P("shard", "expert", None),
            P("shard", "expert", None),
        ),
        check_vma=False,
    )
```

```python
import functools

import jax
import jax.numpy as jnp
from jax import lax
from jax.experimental import pallas as pl
from jax.experimental.pallas import tpu as pltpu
from jax.sharding import PartitionSpec as P

HEADS = 12
EPSILON = 1e-06
CHUNKS = 2
LANES = 128
MIB = 1024 * 1024
BF16 = jnp.bfloat16
F32 = jnp.float32
NN = (((1,), (0,)), ((), ()))
NT = (((1,), (1,)), ((), ()))
TN = (((0,), (0,)), ((), ()))


def dot(a, b, dims=NN):
    return lax.dot_general(a, b, dims, preferred_element_type=F32)


def whole(shape):
    return pl.BlockSpec(shape, lambda *_: (0,) * len(shape), pipeline_mode=pl.Buffered(1))


def call(kernel, grid, in_specs, out_specs, out_shape, scratch, limit):
    return pl.pallas_call(
        kernel,
        grid=grid,
        in_specs=in_specs,
        out_specs=out_specs,
        out_shape=out_shape,
        scratch_shapes=scratch,
        compiler_params=pltpu.CompilerParams(
            vmem_limit_bytes=limit * MIB,
            dimension_semantics=("arbitrary",) * len(grid),
        ),
    )


def normal(value):
    centered = value - jnp.mean(value, -1, keepdims=True)
    inverse = lax.rsqrt(jnp.mean(centered * centered, -1, keepdims=True) + EPSILON)
    return centered * inverse, inverse


def norm_back(grad, gain, unit, inverse):
    scaled = grad * gain
    return inverse * (
        scaled
        - jnp.mean(scaled, -1, keepdims=True)
        - unit * jnp.mean(scaled * unit, -1, keepdims=True)
    )


def one_hot(equal):
    return jnp.where(equal, 1.0, 0.0).astype(BF16)


def padded_rows(source, buffer):
    length = source.shape[1]
    buffer[...] = jnp.zeros_like(buffer)
    buffer[0:length, :] = source[0].astype(buffer.dtype)
    return buffer[...]


def send_images_kernel(codes_ref, source_ref, out_ref, rows):
    images, length, _ = source_ref.shape
    padded = rows.shape[0] // images
    step = pl.program_id(0)

    @pl.when(step == 0)
    def _():
        rows[...] = jnp.zeros_like(rows)
        for image in range(images):
            rows[image * padded : image * padded + length, :] = source_ref[image].astype(F32)

    pick_rows(codes_ref, rows[...].astype(BF16), out_ref, step)


def send_rows_kernel(codes_ref, source_ref, out_ref):
    pick_rows(codes_ref, source_ref[...], out_ref, pl.program_id(0))


def pick_rows(codes_ref, rows, out_ref, step):
    count = out_ref.shape[1]
    tokens = rows.shape[0]
    slot = lax.broadcasted_iota(jnp.int32, (count, tokens), 0) + step * count
    hot = one_hot((slot == codes_ref[0:1, :]) | (slot == codes_ref[1:2, :]))
    out_ref[0] = dot(hot, rows).astype(BF16)


def send(source, codes, experts, count, width):
    tokens = codes.shape[1]
    if source.ndim == 3:
        kernel, scratch = send_images_kernel, [pltpu.VMEM((tokens, width), F32)]
    else:
        kernel, scratch = send_rows_kernel, []
    return call(
        kernel,
        (experts,),
        [whole(codes.shape), whole(source.shape)],
        pl.BlockSpec((1, count, width), lambda e: (e, 0, 0)),
        jax.ShapeDtypeStruct((experts, count, width), BF16),
        scratch,
        40,
    )(codes, source)


def gather_rows(codes, arrays):
    total = None
    for chunk, array in enumerate(arrays):
        slot = lax.broadcasted_iota(jnp.int32, (codes.shape[0], array.shape[0]), 1)
        first = codes[:, 2 * chunk : 2 * chunk + 1]
        second = codes[:, 2 * chunk + 1 : 2 * chunk + 2]
        part = dot(one_hot((slot == first) | (slot == second)), array[...])
        total = part if total is None else total + part
    return total


def attend_kernel(
    tokens_ref, qkv_weight_ref, out_weight_ref, vector_ref,
    qkv_ref, mixed_ref, attended_ref, first_ref, second_ref, buffer,
):
    length = tokens_ref.shape[1]
    padded, width = buffer.shape
    value = padded_rows(tokens_ref, buffer)
    unit, _ = normal(value)
    first = (unit * vector_ref[0:1, :] + vector_ref[1:2, :]).astype(BF16)
    first_ref[0] = first
    qkv_ref[0] = dot(first, qkv_weight_ref[...]).astype(BF16)
    scale = (width // HEADS) ** (-0.5)
    per_tile = LANES * HEADS // width
    lane = lax.broadcasted_iota(jnp.int32, (padded, LANES), 1) // (width // HEADS)
    real = lax.broadcasted_iota(jnp.int32, (padded, padded), 1) < length
    for tile in range(width // LANES):
        at = tile * LANES
        query = qkv_ref[0, :, at : at + LANES]
        keys = qkv_ref[0, :, width + at : width + at + LANES]
        values = qkv_ref[0, :, 2 * width + at : 2 * width + at + LANES]
        result = None
        for head in range(per_tile):
            chosen = jnp.where(lane == head, query.astype(F32) * scale, 0.0).astype(BF16)
            scores = jnp.where(real, dot(chosen, keys, NT), -1e30)
            raised = jnp.exp(scores - jnp.max(scores, -1, keepdims=True))
            probs = raised * (1.0 / jnp.sum(raised, -1, keepdims=True))
            part = dot(probs.astype(BF16), values)
            result = part if result is None else jnp.where(lane == head, part, result)
        mixed_ref[0, :, at : at + LANES] = result.astype(BF16)
    attended = value + dot(mixed_ref[0], out_weight_ref[...])
    attended_ref[0] = attended
    unit, _ = normal(attended)
    second_ref[0] = (unit * vector_ref[2:3, :] + vector_ref[3:4, :]).astype(BF16)


def attend(tokens, weights, vectors, padded):
    images, length, width = tokens.shape
    image = lambda cols: pl.BlockSpec((1, padded, cols), lambda i: (i, 0, 0))
    shape = lambda cols, kind: jax.ShapeDtypeStruct((images, padded, cols), kind)
    return call(
        attend_kernel,
        (images,),
        [
            pl.BlockSpec((1, length, width), lambda i: (i, 0, 0)),
            pl.BlockSpec((width, 3 * width), lambda i: (0, 0), pipeline_mode=pl.Buffered(1)),
            pl.BlockSpec((width, width), lambda i: (0, 3), pipeline_mode=pl.Buffered(1)),
            whole(vectors.shape),
        ],
        [image(3 * width), image(width), image(width), image(width), image(width)],
        [
            shape(3 * width, BF16), shape(width, BF16), shape(width, F32),
            shape(width, BF16), shape(width, BF16),
        ],
        [pltpu.VMEM((padded, width), F32)],
        40,
    )(tokens, weights, weights, vectors)


def gelu_pair(value):
    root = 0.7978845608028654
    cubic = 0.044715
    square = value * value
    bent = jnp.tanh(value * (root + root * cubic * square))
    half = 0.5 + 0.5 * bent
    active = value * half
    slope = half + active * (1.0 - half) * (2.0 * root + 6.0 * root * cubic * square)
    return active, slope


def expert_kernel(experts, block, kept, mine_ref, x_ref, g_ref, up_ref, down_ref, router_ref, *refs):
    (
        active_ref, before_ref, scaled_ref, x_all_ref, logit_ref, out_ref, back_ref,
        out_sum, back_sum, probs_ref,
    ) = refs[kept:]
    step = pl.program_id(0)
    sources, count, width = x_ref.shape
    total = sources * count
    blocks = total // block
    mine = mine_ref[0:1, :]

    @pl.when(step == 0)
    def _():
        out_sum[...] = jnp.zeros_like(out_sum)
        back_sum[...] = jnp.zeros_like(back_sum)
        for source in range(sources):
            rows = slice(source * count, (source + 1) * count)
            x = x_ref[source]
            x_all_ref[0, rows, :] = x
            logits = dot(x, router_ref[...])
            column = lax.broadcasted_iota(jnp.int32, logits.shape, 1)
            logits = jnp.where(column < experts, logits, -1e30)
            raised = jnp.exp(logits - jnp.max(logits, -1, keepdims=True))
            probs = raised / jnp.sum(raised, -1, keepdims=True)
            probs_ref[rows, :] = probs
            gate = jnp.sum(probs * mine, -1, keepdims=True)
            scaled_ref[0, rows, :] = (gate * g_ref[source].astype(F32)).astype(BF16)

    def first_products(index):
        rows = slice(index * block, (index + 1) * block)
        before = dot(x_all_ref[0, rows, :], up_ref[...], NT)
        return before, dot(scaled_ref[0, rows, :], down_ref[...], NT)

    ahead = first_products(0)
    for index in range(blocks):
        rows = slice(index * block, (index + 1) * block)
        before, active_grad = ahead
        if index + 1 < blocks:
            ahead = first_products(index + 1)
        active, slope = gelu_pair(before)
        active = active.astype(BF16)
        before_grad = (active_grad * slope).astype(BF16)
        active_ref[0, rows, :] = active
        before_ref[0, rows, :] = before_grad
        out_sum[rows, :] += dot(active, down_ref[...])
        back_sum[rows, :] += dot(before_grad, up_ref[...])

    @pl.when(step == pl.num_programs(0) - 1)
    def _():
        for source in range(sources):
            rows = slice(source * count, (source + 1) * count)
            made = out_sum[rows, :].astype(BF16).astype(F32)
            probs = probs_ref[rows, :]
            gate = jnp.sum(probs * mine, -1, keepdims=True)
            gate_grad = jnp.sum(made * g_ref[source].astype(F32), -1, keepdims=True)
            logit = (gate_grad * gate * (mine - probs)).astype(BF16)
            logit_ref[0, rows, :] = logit
            out_ref[source] = (gate * made).astype(BF16)
            back_ref[source] = (
                back_sum[rows, :] + dot(logit, router_ref[...], NT)
            ).astype(BF16)


def run_expert(chunk, kept, mine, x, g, up, down, weights, experts):
    sources, count, width = x.shape
    rows = sources * count
    hidden = up.shape[0]
    part = 768
    block = 256
    last = weights.shape[1] // LANES - 1
    chunk_rows = (sources, count, width)
    wide = pl.BlockSpec((1, rows, part), lambda f: (chunk, 0, f))
    weight = pl.BlockSpec((part, width), lambda f: (f, 0))
    slots = pl.BlockSpec(chunk_rows, lambda f: (0, chunk, 0), pipeline_mode=pl.Buffered(1))
    one = lambda cols: pl.BlockSpec(
        (1, rows, cols), lambda f: (chunk, 0, 0), pipeline_mode=pl.Buffered(1)
    )
    made = lambda cols: jax.ShapeDtypeStruct((CHUNKS, rows, cols), BF16)
    return pl.pallas_call(
        functools.partial(expert_kernel, experts, block, len(kept)),
        grid=(hidden // part,),
        in_specs=[
            whole(mine.shape),
            whole(chunk_rows),
            slots,
            weight,
            weight,
            pl.BlockSpec((width, LANES), lambda f: (0, last), pipeline_mode=pl.Buffered(1)),
        ]
        + [pl.BlockSpec(memory_space=pl.ANY)] * len(kept),
        out_specs=[wide, wide, one(width), one(width), one(LANES), slots, whole(chunk_rows)],
        out_shape=[made(hidden), made(hidden), made(width), made(width), made(LANES)]
        + [jax.ShapeDtypeStruct(g.shape, BF16), jax.ShapeDtypeStruct(chunk_rows, BF16)],
        scratch_shapes=[
            pltpu.VMEM((rows, width), F32), pltpu.VMEM((rows, width), F32), pltpu.VMEM((rows, LANES), F32)
        ],
        input_output_aliases={6 + index: index for index in range(len(kept))},
        compiler_params=pltpu.CompilerParams(
            vmem_limit_bytes=56 * MIB, dimension_semantics=("arbitrary",)
        ),
    )(mine, x, g, up, down, weights, *kept)


def attend_back_kernel(*refs):
    codes_ref, *refs = refs
    returned, refs = refs[:CHUNKS], refs[CHUNKS:]
    (
        cotangent_ref, tokens_ref, attended_ref, qkv_ref,
        qkv_weight_ref, out_weight_ref, vector_ref,
        tokens_grad_ref, branch_ref, rows_grad_ref, sums_ref, buffer,
    ) = refs
    length = tokens_ref.shape[1]
    padded, width = buffer.shape

    @pl.when(pl.program_id(0) == 0)
    def _():
        sums_ref[...] = jnp.zeros_like(sums_ref)

    second_grad = gather_rows(codes_ref[0], returned)
    unit, inverse = normal(attended_ref[0])
    sums_ref[2:3, :] += jnp.sum(second_grad * unit, 0, keepdims=True)
    sums_ref[3:4, :] += jnp.sum(second_grad, 0, keepdims=True)
    attended_grad = padded_rows(cotangent_ref, buffer) + norm_back(
        second_grad, vector_ref[2:3, :], unit, inverse
    )
    branch = attended_grad.astype(BF16)
    branch_ref[0] = branch
    mixed_grad = dot(branch, out_weight_ref[...], NT).astype(BF16)
    scale = (width // HEADS) ** (-0.5)
    per_tile = LANES * HEADS // width
    lane = lax.broadcasted_iota(jnp.int32, (padded, LANES), 1) // (width // HEADS)
    real = lax.broadcasted_iota(jnp.int32, (padded, padded), 0) < length
    for tile in range(width // LANES):
        at = tile * LANES
        query = qkv_ref[0, :, at : at + LANES].astype(F32) * scale
        keys = qkv_ref[0, :, width + at : width + at + LANES]
        values = qkv_ref[0, :, 2 * width + at : 2 * width + at + LANES]
        keys_scaled = keys.astype(F32) * scale
        result = mixed_grad[:, at : at + LANES].astype(F32)
        grads = [None, None, None]
        for head in range(per_tile):
            own = lane == head
            own_query = jnp.where(own, query, 0.0).astype(BF16)
            own_keys = jnp.where(own, keys_scaled, 0.0).astype(BF16)
            own_result = jnp.where(own, result, 0.0).astype(BF16)
            scores = jnp.where(real, dot(keys, own_query, NT), -1e30)
            raised = jnp.exp(scores - jnp.max(scores, 0, keepdims=True))
            probs = raised * (1.0 / jnp.sum(raised, 0, keepdims=True))
            prob_grad = dot(values, own_result, NT)
            score_grad = (
                probs * (prob_grad - jnp.sum(probs * prob_grad, 0, keepdims=True))
            ).astype(BF16)
            parts = (
                dot(score_grad, own_keys, TN),
                dot(score_grad, own_query),
                dot(probs.astype(BF16), own_result),
            )
            grads = [part if old is None else old + part for old, part in zip(grads, parts)]
        for index, grad in enumerate(grads):
            start = index * width + at
            rows_grad_ref[0, :, start : start + LANES] = grad.astype(BF16)
    first_grad = dot(rows_grad_ref[0], qkv_weight_ref[...], NT)
    unit, inverse = normal(padded_rows(tokens_ref, buffer))
    sums_ref[0:1, :] += jnp.sum(first_grad * unit, 0, keepdims=True)
    sums_ref[1:2, :] += jnp.sum(first_grad, 0, keepdims=True)
    tokens_grad = attended_grad + norm_back(first_grad, vector_ref[0:1, :], unit, inverse)
    tokens_grad_ref[0] = tokens_grad[0:length, :].astype(BF16)


def attend_back(codes, returned, cotangent, tokens, attended, qkv, weights, vectors):
    images, length, width = tokens.shape
    padded = attended.shape[1]
    image = lambda rows, cols: pl.BlockSpec((1, rows, cols), lambda i: (i, 0, 0))
    return call(
        attend_back_kernel,
        (images,),
        [image(padded, codes.shape[2])]
        + [whole(array.shape) for array in returned]
        + [
            image(length, width), image(length, width), image(padded, width), image(padded, 3 * width),
            pl.BlockSpec((width, 3 * width), lambda i: (0, 0), pipeline_mode=pl.Buffered(1)),
            pl.BlockSpec((width, width), lambda i: (0, 3), pipeline_mode=pl.Buffered(1)),
            whole(vectors.shape),
        ],
        [image(length, width), image(padded, width), image(padded, 3 * width), whole((8, width))],
        [
            jax.ShapeDtypeStruct((images, length, width), BF16),
            jax.ShapeDtypeStruct((images, padded, width), BF16),
            jax.ShapeDtypeStruct((images, padded, 3 * width), BF16),
            jax.ShapeDtypeStruct((8, width), F32),
        ],
        [pltpu.VMEM((padded, width), F32)],
        48,
    )(codes, *returned, cotangent, tokens, attended, qkv, weights, weights, vectors)


def combine_kernel(codes_ref, *refs):
    *returned, attended_ref, out_ref = refs
    total = attended_ref[0] + gather_rows(codes_ref[0], returned)
    out_ref[0] = total[0 : out_ref.shape[1], :].astype(BF16)


def combine(codes, returned, attended, length):
    images, padded, width = attended.shape
    image = lambda rows, cols: pl.BlockSpec((1, rows, cols), lambda i: (i, 0, 0))
    return call(
        combine_kernel,
        (images,),
        [image(padded, codes.shape[2])]
        + [whole(array.shape) for array in returned]
        + [image(padded, width)],
        image(length, width),
        jax.ShapeDtypeStruct((images, length, width), BF16),
        [],
        40,
    )(codes, *returned, attended)


def sum_shards(array):
    size = lax.axis_size("shard")
    rows, cols = array.shape
    pairs = size // 2
    me = lax.axis_index("shard")
    blocks = array.reshape(pairs, 2, rows // size, cols)
    take = lambda core: lax.dynamic_index_in_dim(blocks, core, 1, keepdims=False)
    other = lax.ppermute(take(1 - me % 2), "shard", [(s, s ^ 1) for s in range(size)])
    halves = take(me % 2).astype(F32) + other.astype(F32)
    sent = halves.astype(BF16)
    at = me // 2
    total = lax.dynamic_index_in_dim(halves, at, 0, keepdims=False)
    for shift in range(1, pairs):
        part = lax.dynamic_index_in_dim(sent, (at + shift) % pairs, 0, keepdims=False)
        moves = [(s, (s // 2 + shift) % pairs * 2 + s % 2) for s in range(size)]
        total = total + lax.ppermute(part, "shard", moves).astype(F32)
    return total.astype(BF16)


def exchange(array):
    return lax.all_to_all(array, "expert", split_axis=0, concat_axis=0, tiled=True)


def shards(
    tokens,
    ln1_gain,
    ln1_bias,
    qkv_weight,
    out_weight,
    ln2_gain,
    ln2_bias,
    router_weight,
    up_weight,
    down_weight,
    routes,
    slots,
    keep,
    cotangent,
):
    images, length, width = tokens.shape
    rows = images * length
    experts = lax.axis_size("expert")
    assert up_weight.shape[1] == 1 and router_weight.shape[1] == experts
    capacity = max(4, 5 * rows // (2 * experts))
    count = -(-capacity // (16 * CHUNKS)) * 16
    padded = -(-length // 16) * 16

    columns = experts + 4
    spare = -columns % LANES
    small = jnp.concatenate(
        [router_weight, jnp.stack([ln1_gain, ln1_bias, ln2_gain, ln2_bias], 1)], 1
    )
    packed = jnp.concatenate(
        [qkv_weight, out_weight, jnp.pad(small, ((0, 0), (0, spare)))], 1
    )
    weights = lax.all_gather(packed, "shard", axis=0, tiled=True)
    vectors = jnp.pad(
        weights[:, 4 * width + experts : 4 * width + columns].T.astype(F32), ((0, 4), (0, 0))
    )

    chunk_codes = []
    for chunk in range(CHUNKS):
        place = slots - chunk * count
        here = (keep > 0) & (place >= 0) & (place < count)
        chunk_codes.append(jnp.where(here, routes * count + place, -1))
    codes = jnp.pad(
        jnp.concatenate(chunk_codes, -1),
        ((0, 0), (0, padded - length), (0, 0)),
        constant_values=-1,
    )
    flat_codes = codes.reshape(images * padded, 2 * CHUNKS).T
    row_codes = [flat_codes[2 * chunk : 2 * chunk + 2] for chunk in range(CHUNKS)]

    all_codes = jnp.pad(
        jnp.where(keep > 0, routes * (CHUNKS * count) + slots, -1),
        ((0, 0), (0, padded - length), (0, 0)),
        constant_values=-1,
    )
    g_codes = all_codes.reshape(images * padded, 2).T
    g_sent = send(cotangent, g_codes, experts, CHUNKS * count, width)
    g_sent, tokens_in = lax.optimization_barrier((g_sent, tokens))
    g_here = exchange(g_sent)

    up = lax.all_gather(up_weight.reshape(-1, width), "shard", axis=0, tiled=True)
    down = lax.all_gather(down_weight.reshape(-1, width), "shard", axis=0, tiled=True)

    qkv, mixed, attended, first, second = attend(tokens_in, weights, vectors, padded)
    flat_second = second.reshape(images * padded, width)
    mine = (
        lax.broadcasted_iota(jnp.int32, (8, LANES), 1) == lax.axis_index("expert")
    ).astype(F32)

    back_here, kept = [], []
    for chunk in range(CHUNKS):
        x = exchange(send(flat_second, row_codes[chunk], experts, count, width))
        *kept, back = run_expert(chunk, kept, mine, x, g_here, up, down, weights, experts)
        back_here.append(back)
    *kept, out_here = kept
    active, before_grad, scaled, x_all, logit = [
        array.reshape(CHUNKS * experts * count, -1) for array in kept
    ]

    returned = [exchange(array).reshape(experts * count, width) for array in back_here]
    out_here, returned = lax.optimization_barrier((out_here, returned))
    out_returned = exchange(out_here).reshape(experts * CHUNKS * count, width)

    down_full = dot(active, scaled, TN).astype(BF16)
    up_full = dot(before_grad, x_all, TN).astype(BF16)
    router_full = dot(x_all, logit, TN)
    down_full, up_full, router_full, returned = lax.optimization_barrier(
        (down_full, up_full, router_full, returned)
    )
    down_grad = lax.psum_scatter(down_full, "shard", scatter_dimension=0, tiled=True)
    up_grad = lax.psum_scatter(up_full, "shard", scatter_dimension=0, tiled=True)

    tokens_grad, branch, rows_grad, sums = attend_back(
        codes, returned, cotangent, tokens, attended, qkv, weights, vectors
    )
    flat = lambda array: array.reshape(images * padded, -1)
    qkv_full = dot(flat(first), flat(rows_grad), TN)
    out_full = dot(flat(mixed), flat(branch), TN)
    small_full = jnp.concatenate([router_full[:, :experts], sums[0:4].T], 1)
    layer = jnp.concatenate(
        [qkv_full, out_full, jnp.pad(small_full, ((0, 0), (0, spare)))], 1
    ).astype(BF16)
    layer = sum_shards(layer)
    layer, up_grad, down_grad = lax.optimization_barrier((layer, up_grad, down_grad))
    layer = lax.psum(layer, "expert").astype(F32)
    block_out = combine(all_codes, [out_returned], attended, length)
    tail = 4 * width + experts
    return (
        block_out,
        tokens_grad,
        layer[:, tail],
        layer[:, tail + 1],
        layer[:, : 3 * width],
        layer[:, 3 * width : 4 * width],
        layer[:, tail + 2],
        layer[:, tail + 3],
        layer[:, 4 * width : tail],
        up_grad.astype(F32)[:, None, :],
        down_grad.astype(F32)[:, None, :],
    )


def solution(mesh):
    placed = (
        P(("expert", "shard"), None, None),
        P("shard"),
        P("shard"),
        P("shard", None),
        P("shard", None),
        P("shard"),
        P("shard"),
        P("shard", None),
        P("shard", "expert", None),
        P("shard", "expert", None),
        P(("expert", "shard"), None, None),
        P(("expert", "shard"), None, None),
        P(("expert", "shard"), None, None),
        P(("expert", "shard"), None, None),
    )
    return jax.shard_map(
        shards,
        mesh=mesh,
        in_specs=placed,
        out_specs=(
            P(("expert", "shard"), None, None),
            P(("expert", "shard"), None, None),
            P("shard"),
            P("shard"),
            P("shard", None),
            P("shard", None),
            P("shard"),
            P("shard"),
            P("shard", None),
            P("shard", "expert", None),
            P("shard", "expert", None),
        ),
        check_vma=False,
    )
```

```python
import functools

import jax
import jax.numpy as jnp
from jax import lax
from jax.experimental import pallas as pl
from jax.experimental.pallas import tpu as pltpu
from jax.sharding import PartitionSpec as P

HEADS = 12
EPSILON = 1e-06
CHUNKS = 2
LANES = 128
MIB = 1024 * 1024
BF16 = jnp.bfloat16
F32 = jnp.float32
NN = (((1,), (0,)), ((), ()))
NT = (((1,), (1,)), ((), ()))
TN = (((0,), (0,)), ((), ()))


def dot(a, b, dims=NN):
    return lax.dot_general(a, b, dims, preferred_element_type=F32)


def whole(shape):
    return pl.BlockSpec(shape, lambda *_: (0,) * len(shape), pipeline_mode=pl.Buffered(1))


def cost(products, moved, powers=0):
    return pl.CostEstimate(flops=2 * products, transcendentals=powers, bytes_accessed=moved)


def call(kernel, grid, in_specs, out_specs, out_shape, scratch, limit, estimate):
    return pl.pallas_call(
        kernel,
        grid=grid,
        in_specs=in_specs,
        out_specs=out_specs,
        out_shape=out_shape,
        scratch_shapes=scratch,
        cost_estimate=estimate,
        compiler_params=pltpu.CompilerParams(
            vmem_limit_bytes=limit * MIB,
            dimension_semantics=("arbitrary",) * len(grid),
        ),
    )


def normal(value):
    centered = value - jnp.mean(value, -1, keepdims=True)
    inverse = lax.rsqrt(jnp.mean(centered * centered, -1, keepdims=True) + EPSILON)
    return centered * inverse, inverse


def norm_back(grad, gain, unit, inverse):
    scaled = grad * gain
    return inverse * (
        scaled
        - jnp.mean(scaled, -1, keepdims=True)
        - unit * jnp.mean(scaled * unit, -1, keepdims=True)
    )


def one_hot(equal):
    return jnp.where(equal, 1.0, 0.0).astype(BF16)


def padded_rows(source, buffer):
    group, length, _ = source.shape
    padded = buffer.shape[0] // group
    buffer[...] = jnp.zeros_like(buffer)
    for image in range(group):
        buffer[image * padded : image * padded + length, :] = source[image].astype(buffer.dtype)
    return buffer[...]


def group_of(images):
    return 2 if images % 2 == 0 else 1


def stacked(tile, lane, heads):
    return jnp.concatenate(
        [jnp.where(lane == head, tile, 0.0) for head in range(heads)], 0
    ).astype(BF16)


def unstacked(rows, lane, heads):
    count = rows.shape[0] // heads
    result = rows[0:count, :]
    for head in range(1, heads):
        result = jnp.where(lane == head, rows[head * count : (head + 1) * count, :], result)
    return result


def send_images_kernel(codes_ref, source_ref, out_ref, rows):
    images, length, _ = source_ref.shape
    padded = rows.shape[0] // images
    step = pl.program_id(0)

    @pl.when(step == 0)
    def _():
        rows[...] = jnp.zeros_like(rows)
        for image in range(images):
            rows[image * padded : image * padded + length, :] = source_ref[image].astype(F32)

    pick_rows(codes_ref, rows[...].astype(BF16), out_ref, step)


def send_rows_kernel(codes_ref, source_ref, out_ref):
    pick_rows(codes_ref, source_ref[...], out_ref, pl.program_id(0))


def pick_rows(codes_ref, rows, out_ref, step):
    count = out_ref.shape[1]
    tokens = rows.shape[0]
    slot = lax.broadcasted_iota(jnp.int32, (count, tokens), 0) + step * count
    hot = one_hot((slot == codes_ref[0:1, :]) | (slot == codes_ref[1:2, :]))
    out_ref[0] = dot(hot, rows).astype(BF16)


def send(source, codes, experts, count, width):
    tokens = codes.shape[1]
    if source.ndim == 3:
        kernel, scratch = send_images_kernel, [pltpu.VMEM((tokens, width), F32)]
    else:
        kernel, scratch = send_rows_kernel, []
    return call(
        kernel,
        (experts,),
        [whole(codes.shape), whole(source.shape)],
        pl.BlockSpec((1, count, width), lambda e: (e, 0, 0)),
        jax.ShapeDtypeStruct((experts, count, width), BF16),
        scratch,
        40,
        cost(experts * count * tokens * width, 2 * (tokens + experts * count) * width),
    )(codes, source)


def gather_rows(codes, arrays):
    total = None
    for chunk, array in enumerate(arrays):
        slot = lax.broadcasted_iota(jnp.int32, (codes.shape[0], array.shape[0]), 1)
        first = codes[:, 2 * chunk : 2 * chunk + 1]
        second = codes[:, 2 * chunk + 1 : 2 * chunk + 2]
        part = dot(one_hot((slot == first) | (slot == second)), array[...])
        total = part if total is None else total + part
    return total


def attend_kernel(
    tokens_ref, qkv_weight_ref, out_weight_ref, vector_ref,
    qkv_ref, mixed_ref, attended_ref, first_ref, second_ref, buffer,
):
    group, length, width = tokens_ref.shape
    padded = buffer.shape[0] // group
    value = padded_rows(tokens_ref, buffer)
    unit, _ = normal(value)
    first = (unit * vector_ref[0:1, :] + vector_ref[1:2, :]).astype(BF16)
    first_ref[...] = first.reshape(group, padded, width)
    qkv = dot(first, qkv_weight_ref[...]).astype(BF16)
    qkv_ref[...] = qkv.reshape(group, padded, 3 * width)
    scale = (width // HEADS) ** (-0.5)
    heads = LANES * HEADS // width
    lane = lax.broadcasted_iota(jnp.int32, (padded, LANES), 1) // (width // HEADS)
    real = lax.broadcasted_iota(jnp.int32, (heads * padded, padded), 1) < length
    for image in range(group):
        for at in range(0, width, LANES):
            query = qkv_ref[image, :, at : at + LANES].astype(F32) * scale
            keys = qkv_ref[image, :, width + at : width + at + LANES]
            values = qkv_ref[image, :, 2 * width + at : 2 * width + at + LANES]
            scores = jnp.where(real, dot(stacked(query, lane, heads), keys, NT), -1e30)
            raised = jnp.exp(scores - jnp.max(scores, -1, keepdims=True))
            probs = raised * (1.0 / jnp.sum(raised, -1, keepdims=True))
            result = unstacked(dot(probs.astype(BF16), values), lane, heads)
            mixed_ref[image, :, at : at + LANES] = result.astype(BF16)
    mixed = mixed_ref[...].reshape(group * padded, width)
    attended = buffer[...] + dot(mixed, out_weight_ref[...])
    attended_ref[...] = attended.reshape(group, padded, width)
    unit, _ = normal(attended)
    second = (unit * vector_ref[2:3, :] + vector_ref[3:4, :]).astype(BF16)
    second_ref[...] = second.reshape(group, padded, width)


def attend(tokens, weights, vectors, padded):
    images, length, width = tokens.shape
    group = group_of(images)
    rows = images * padded
    image = lambda cols: pl.BlockSpec((group, padded, cols), lambda i: (i, 0, 0))
    shape = lambda cols, kind: jax.ShapeDtypeStruct((images, padded, cols), kind)
    return call(
        attend_kernel,
        (images // group,),
        [
            pl.BlockSpec((group, length, width), lambda i: (i, 0, 0)),
            pl.BlockSpec((width, 3 * width), lambda i: (0, 0), pipeline_mode=pl.Buffered(1)),
            pl.BlockSpec((width, width), lambda i: (0, 3), pipeline_mode=pl.Buffered(1)),
            whole(vectors.shape),
        ],
        [image(3 * width), image(width), image(width), image(width), image(width)],
        [
            shape(3 * width, BF16), shape(width, BF16), shape(width, F32),
            shape(width, BF16), shape(width, BF16),
        ],
        [pltpu.VMEM((group * padded, width), F32)],
        44,
        cost(
            rows * width * (4 * width + 4 * padded),
            rows * width * 18 + width * width * 8,
            rows * padded * HEADS,
        ),
    )(tokens, weights, weights, vectors)


def gelu_pair(value):
    root = 0.7978845608028654
    cubic = 0.044715
    square = value * value
    bent = jnp.tanh(value * (root + root * cubic * square))
    half = 0.5 + 0.5 * bent
    active = value * half
    slope = half + active * (1.0 - half) * (2.0 * root + 6.0 * root * cubic * square)
    return active, slope


def expert_kernel(experts, block, kept, mine_ref, x_ref, g_ref, up_ref, down_ref, router_ref, *refs):
    (
        active_ref, before_ref, scaled_ref, x_all_ref, logit_ref, out_ref, back_ref,
        out_sum, back_sum, probs_ref,
    ) = refs[kept:]
    step = pl.program_id(0)
    sources, count, width = x_ref.shape
    total = sources * count
    blocks = total // block
    mine = mine_ref[0:1, :]

    @pl.when(step == 0)
    def _():
        out_sum[...] = jnp.zeros_like(out_sum)
        back_sum[...] = jnp.zeros_like(back_sum)
        for source in range(sources):
            rows = slice(source * count, (source + 1) * count)
            x = x_ref[source]
            x_all_ref[0, rows, :] = x
            logits = dot(x, router_ref[...])
            column = lax.broadcasted_iota(jnp.int32, logits.shape, 1)
            logits = jnp.where(column < experts, logits, -1e30)
            raised = jnp.exp(logits - jnp.max(logits, -1, keepdims=True))
            probs = raised / jnp.sum(raised, -1, keepdims=True)
            probs_ref[rows, :] = probs
            gate = jnp.sum(probs * mine, -1, keepdims=True)
            scaled_ref[0, rows, :] = (gate * g_ref[source].astype(F32)).astype(BF16)

    def first_products(index):
        rows = slice(index * block, (index + 1) * block)
        before = dot(x_all_ref[0, rows, :], up_ref[...], NT)
        return before, dot(scaled_ref[0, rows, :], down_ref[...], NT)

    ahead = first_products(0)
    for index in range(blocks):
        rows = slice(index * block, (index + 1) * block)
        before, active_grad = ahead
        if index + 1 < blocks:
            ahead = first_products(index + 1)
        active, slope = gelu_pair(before)
        active = active.astype(BF16)
        before_grad = (active_grad * slope).astype(BF16)
        active_ref[0, rows, :] = active
        before_ref[0, rows, :] = before_grad
        out_sum[rows, :] += dot(active, down_ref[...])
        back_sum[rows, :] += dot(before_grad, up_ref[...])

    @pl.when(step == pl.num_programs(0) - 1)
    def _():
        for source in range(sources):
            rows = slice(source * count, (source + 1) * count)
            made = out_sum[rows, :].astype(BF16).astype(F32)
            probs = probs_ref[rows, :]
            gate = jnp.sum(probs * mine, -1, keepdims=True)
            gate_grad = jnp.sum(made * g_ref[source].astype(F32), -1, keepdims=True)
            logit = (gate_grad * gate * (mine - probs)).astype(BF16)
            logit_ref[0, rows, :] = logit
            out_ref[source] = (gate * made).astype(BF16)
            back_ref[source] = (
                back_sum[rows, :] + dot(logit, router_ref[...], NT)
            ).astype(BF16)


def run_expert(chunk, kept, mine, x, g, up, down, weights, experts):
    sources, count, width = x.shape
    rows = sources * count
    hidden = up.shape[0]
    part = 768
    block = 256
    last = weights.shape[1] // LANES - 1
    chunk_rows = (sources, count, width)
    wide = pl.BlockSpec((1, rows, part), lambda f: (chunk, 0, f))
    weight = pl.BlockSpec((part, width), lambda f: (f, 0))
    slots = pl.BlockSpec(chunk_rows, lambda f: (0, chunk, 0), pipeline_mode=pl.Buffered(1))
    one = lambda cols: pl.BlockSpec(
        (1, rows, cols), lambda f: (chunk, 0, 0), pipeline_mode=pl.Buffered(1)
    )
    made = lambda cols: jax.ShapeDtypeStruct((CHUNKS, rows, cols), BF16)
    return pl.pallas_call(
        functools.partial(expert_kernel, experts, block, len(kept)),
        grid=(hidden // part,),
        in_specs=[
            whole(mine.shape),
            whole(chunk_rows),
            slots,
            weight,
            weight,
            pl.BlockSpec((width, LANES), lambda f: (0, last), pipeline_mode=pl.Buffered(1)),
        ]
        + [pl.BlockSpec(memory_space=pl.ANY)] * len(kept),
        out_specs=[wide, wide, one(width), one(width), one(LANES), slots, whole(chunk_rows)],
        out_shape=[made(hidden), made(hidden), made(width), made(width), made(LANES)]
        + [jax.ShapeDtypeStruct(g.shape, BF16), jax.ShapeDtypeStruct(chunk_rows, BF16)],
        scratch_shapes=[
            pltpu.VMEM((rows, width), F32), pltpu.VMEM((rows, width), F32), pltpu.VMEM((rows, LANES), F32)
        ],
        cost_estimate=cost(4 * rows * width * hidden, 8 * rows * hidden, rows * hidden),
        input_output_aliases={6 + index: index for index in range(len(kept))},
        compiler_params=pltpu.CompilerParams(
            vmem_limit_bytes=56 * MIB, dimension_semantics=("arbitrary",)
        ),
    )(mine, x, g, up, down, weights, *kept)


def attend_back_kernel(*refs):
    codes_ref, *refs = refs
    returned, refs = refs[:CHUNKS], refs[CHUNKS:]
    (
        cotangent_ref, tokens_ref, attended_ref, qkv_ref,
        qkv_weight_ref, out_weight_ref, vector_ref,
        tokens_grad_ref, branch_ref, rows_grad_ref, sums_ref, buffer, mixed_grad_ref,
    ) = refs
    group, length, width = tokens_ref.shape
    padded = buffer.shape[0] // group

    @pl.when(pl.program_id(0) == 0)
    def _():
        sums_ref[...] = jnp.zeros_like(sums_ref)

    codes = codes_ref[...].reshape(group * padded, codes_ref.shape[2])
    second_grad = gather_rows(codes, returned)
    unit, inverse = normal(attended_ref[...].reshape(group * padded, width))
    sums_ref[2:3, :] += jnp.sum(second_grad * unit, 0, keepdims=True)
    sums_ref[3:4, :] += jnp.sum(second_grad, 0, keepdims=True)
    attended_grad = padded_rows(cotangent_ref, buffer) + norm_back(
        second_grad, vector_ref[2:3, :], unit, inverse
    )
    buffer[...] = attended_grad
    branch = attended_grad.astype(BF16)
    branch_ref[...] = branch.reshape(group, padded, width)
    mixed_grad_ref[...] = (
        dot(branch, out_weight_ref[...], NT).astype(BF16).reshape(group, padded, width)
    )
    scale = (width // HEADS) ** (-0.5)
    heads = LANES * HEADS // width
    lane = lax.broadcasted_iota(jnp.int32, (padded, LANES), 1) // (width // HEADS)
    real = lax.broadcasted_iota(jnp.int32, (padded, heads * padded), 0) < length
    for image in range(group):
        for at in range(0, width, LANES):
            query = qkv_ref[image, :, at : at + LANES].astype(F32) * scale
            keys = qkv_ref[image, :, width + at : width + at + LANES]
            values = qkv_ref[image, :, 2 * width + at : 2 * width + at + LANES]
            result = mixed_grad_ref[image, :, at : at + LANES].astype(F32)
            queries = stacked(query, lane, heads)
            results = stacked(result, lane, heads)
            scores = jnp.where(real, dot(keys, queries, NT), -1e30)
            prob_grad = dot(values, results, NT)
            raised = jnp.exp(scores - jnp.max(scores, 0, keepdims=True))
            probs = raised * (1.0 / jnp.sum(raised, 0, keepdims=True))
            score_grad = (
                probs * (prob_grad - jnp.sum(probs * prob_grad, 0, keepdims=True))
            ).astype(BF16)
            keys_scaled = (keys.astype(F32) * scale).astype(BF16)
            grads = (
                unstacked(dot(score_grad, keys_scaled, TN), lane, heads),
                dot(score_grad, queries),
                dot(probs.astype(BF16), results),
            )
            for index, grad in enumerate(grads):
                start = index * width + at
                rows_grad_ref[image, :, start : start + LANES] = grad.astype(BF16)
    rows_grad = rows_grad_ref[...].reshape(group * padded, 3 * width)
    first_grad = dot(rows_grad, qkv_weight_ref[...], NT)
    attended_grad = buffer[...]
    unit, inverse = normal(padded_rows(tokens_ref, buffer))
    sums_ref[0:1, :] += jnp.sum(first_grad * unit, 0, keepdims=True)
    sums_ref[1:2, :] += jnp.sum(first_grad, 0, keepdims=True)
    tokens_grad = attended_grad + norm_back(first_grad, vector_ref[0:1, :], unit, inverse)
    for image in range(group):
        tokens_grad_ref[image] = tokens_grad[
            image * padded : image * padded + length, :
        ].astype(BF16)


def attend_back(codes, returned, cotangent, tokens, attended, qkv, weights, vectors):
    images, length, width = tokens.shape
    padded = attended.shape[1]
    group = group_of(images)
    rows = images * padded
    image = lambda count, cols: pl.BlockSpec((group, count, cols), lambda i: (i, 0, 0))
    return call(
        attend_back_kernel,
        (images // group,),
        [image(padded, codes.shape[2])]
        + [whole(array.shape) for array in returned]
        + [
            image(length, width), image(length, width), image(padded, width), image(padded, 3 * width),
            pl.BlockSpec((width, 3 * width), lambda i: (0, 0), pipeline_mode=pl.Buffered(1)),
            pl.BlockSpec((width, width), lambda i: (0, 3), pipeline_mode=pl.Buffered(1)),
            whole(vectors.shape),
        ],
        [image(length, width), image(padded, width), image(padded, 3 * width), whole((8, width))],
        [
            jax.ShapeDtypeStruct((images, length, width), BF16),
            jax.ShapeDtypeStruct((images, padded, width), BF16),
            jax.ShapeDtypeStruct((images, padded, 3 * width), BF16),
            jax.ShapeDtypeStruct((8, width), F32),
        ],
        [pltpu.VMEM((group * padded, width), F32), pltpu.VMEM((group, padded, width), BF16)],
        56,
        cost(
            rows * width * (4 * width + 10 * padded + CHUNKS * returned[0].shape[0]),
            rows * width * 24 + width * (width * 8 + 4 * returned[0].shape[0]),
            rows * padded * HEADS,
        ),
    )(codes, *returned, cotangent, tokens, attended, qkv, weights, weights, vectors)


def combine_kernel(codes_ref, *refs):
    *returned, attended_ref, out_ref = refs
    group, padded, width = attended_ref.shape
    codes = codes_ref[...].reshape(group * padded, codes_ref.shape[2])
    total = attended_ref[...].reshape(group * padded, width) + gather_rows(codes, returned)
    for image in range(group):
        at = image * padded
        out_ref[image] = total[at : at + out_ref.shape[1], :].astype(BF16)


def combine(codes, returned, attended, length):
    images, padded, width = attended.shape
    group = group_of(images)
    image = lambda rows, cols: pl.BlockSpec((group, rows, cols), lambda i: (i, 0, 0))
    return call(
        combine_kernel,
        (images // group,),
        [image(padded, codes.shape[2])]
        + [whole(array.shape) for array in returned]
        + [image(padded, width)],
        image(length, width),
        jax.ShapeDtypeStruct((images, length, width), BF16),
        [],
        40,
        cost(
            images * padded * width * sum(array.shape[0] for array in returned),
            images * padded * width * 8,
        ),
    )(codes, *returned, attended)


def sum_shards(array):
    size = lax.axis_size("shard")
    rows, cols = array.shape
    pairs = size // 2
    me = lax.axis_index("shard")
    blocks = array.reshape(pairs, 2, rows // size, cols)
    take = lambda core: lax.dynamic_index_in_dim(blocks, core, 1, keepdims=False)
    other = lax.ppermute(take(1 - me % 2), "shard", [(s, s ^ 1) for s in range(size)])
    halves = take(me % 2).astype(F32) + other.astype(F32)
    sent = halves.astype(BF16)
    at = me // 2
    total = lax.dynamic_index_in_dim(halves, at, 0, keepdims=False)
    for shift in range(1, pairs):
        part = lax.dynamic_index_in_dim(sent, (at + shift) % pairs, 0, keepdims=False)
        moves = [(s, (s // 2 + shift) % pairs * 2 + s % 2) for s in range(size)]
        total = total + lax.ppermute(part, "shard", moves).astype(F32)
    return total.astype(BF16)


def sum_experts(array):
    experts = lax.axis_size("expert")
    rows, cols = array.shape
    parts = exchange(array.reshape(experts, rows // experts, cols))
    share = jnp.sum(parts.astype(F32), 0).astype(BF16)
    return lax.all_gather(share, "expert", axis=0, tiled=True).astype(F32)


def exchange(array):
    return lax.all_to_all(array, "expert", split_axis=0, concat_axis=0, tiled=True)


def shards(
    tokens,
    ln1_gain,
    ln1_bias,
    qkv_weight,
    out_weight,
    ln2_gain,
    ln2_bias,
    router_weight,
    up_weight,
    down_weight,
    routes,
    slots,
    keep,
    cotangent,
):
    images, length, width = tokens.shape
    rows = images * length
    experts = lax.axis_size("expert")
    assert up_weight.shape[1] == 1 and router_weight.shape[1] == experts
    capacity = max(4, 5 * rows // (2 * experts))
    count = -(-capacity // (16 * CHUNKS)) * 16
    padded = -(-length // 16) * 16

    columns = experts + 4
    spare = -columns % LANES
    small = jnp.concatenate(
        [router_weight, jnp.stack([ln1_gain, ln1_bias, ln2_gain, ln2_bias], 1)], 1
    )
    packed = jnp.concatenate(
        [qkv_weight, out_weight, jnp.pad(small, ((0, 0), (0, spare)))], 1
    )
    weights = lax.all_gather(packed, "shard", axis=0, tiled=True)
    vectors = jnp.pad(
        weights[:, 4 * width + experts : 4 * width + columns].T.astype(F32), ((0, 4), (0, 0))
    )

    chunk_codes = []
    for chunk in range(CHUNKS):
        place = slots - chunk * count
        here = (keep > 0) & (place >= 0) & (place < count)
        chunk_codes.append(jnp.where(here, routes * count + place, -1))
    codes = jnp.pad(
        jnp.concatenate(chunk_codes, -1),
        ((0, 0), (0, padded - length), (0, 0)),
        constant_values=-1,
    )
    flat_codes = codes.reshape(images * padded, 2 * CHUNKS).T
    row_codes = [flat_codes[2 * chunk : 2 * chunk + 2] for chunk in range(CHUNKS)]

    all_codes = jnp.pad(
        jnp.where(keep > 0, routes * (CHUNKS * count) + slots, -1),
        ((0, 0), (0, padded - length), (0, 0)),
        constant_values=-1,
    )
    g_codes = all_codes.reshape(images * padded, 2).T
    g_sent = send(cotangent, g_codes, experts, CHUNKS * count, width)
    g_sent, tokens_in = lax.optimization_barrier((g_sent, tokens))
    g_here = exchange(g_sent)

    up = lax.all_gather(up_weight.reshape(-1, width), "shard", axis=0, tiled=True)
    down = lax.all_gather(down_weight.reshape(-1, width), "shard", axis=0, tiled=True)

    qkv, mixed, attended, first, second = attend(tokens_in, weights, vectors, padded)
    flat_second = second.reshape(images * padded, width)
    mine = (
        lax.broadcasted_iota(jnp.int32, (8, LANES), 1) == lax.axis_index("expert")
    ).astype(F32)

    back_here, kept = [], []
    for chunk in range(CHUNKS):
        x = exchange(send(flat_second, row_codes[chunk], experts, count, width))
        *kept, back = run_expert(chunk, kept, mine, x, g_here, up, down, weights, experts)
        back_here.append(back)
    *kept, out_here = kept
    active, before_grad, scaled, x_all, logit = [
        array.reshape(CHUNKS * experts * count, -1) for array in kept
    ]

    returned = [exchange(array).reshape(experts * count, width) for array in back_here]
    out_here, returned = lax.optimization_barrier((out_here, returned))
    out_returned = exchange(out_here).reshape(experts * CHUNKS * count, width)

    down_full = dot(active, scaled, TN).astype(BF16)
    up_full = dot(before_grad, x_all, TN).astype(BF16)
    router_full = dot(x_all, logit, TN)
    down_full, up_full, router_full, returned = lax.optimization_barrier(
        (down_full, up_full, router_full, returned)
    )
    down_grad = lax.psum_scatter(down_full, "shard", scatter_dimension=0, tiled=True)
    up_grad = lax.psum_scatter(up_full, "shard", scatter_dimension=0, tiled=True)

    tokens_grad, branch, rows_grad, sums = attend_back(
        codes, returned, cotangent, tokens, attended, qkv, weights, vectors
    )
    flat = lambda array: array.reshape(images * padded, -1)
    qkv_full = dot(flat(first), flat(rows_grad), TN)
    out_full = dot(flat(mixed), flat(branch), TN)
    small_full = jnp.concatenate([router_full[:, :experts], sums[0:4].T], 1)
    layer = jnp.concatenate(
        [qkv_full, out_full, jnp.pad(small_full, ((0, 0), (0, spare)))], 1
    ).astype(BF16)
    layer = sum_shards(layer)
    layer, out_returned = lax.optimization_barrier((layer, out_returned))
    layer = sum_experts(layer)
    block_out = combine(all_codes, [out_returned], attended, length)
    tail = 4 * width + experts
    return (
        block_out,
        tokens_grad,
        layer[:, tail],
        layer[:, tail + 1],
        layer[:, : 3 * width],
        layer[:, 3 * width : 4 * width],
        layer[:, tail + 2],
        layer[:, tail + 3],
        layer[:, 4 * width : tail],
        up_grad.astype(F32)[:, None, :],
        down_grad.astype(F32)[:, None, :],
    )


def solution(mesh):
    placed = (
        P(("expert", "shard"), None, None),
        P("shard"),
        P("shard"),
        P("shard", None),
        P("shard", None),
        P("shard"),
        P("shard"),
        P("shard", None),
        P("shard", "expert", None),
        P("shard", "expert", None),
        P(("expert", "shard"), None, None),
        P(("expert", "shard"), None, None),
        P(("expert", "shard"), None, None),
        P(("expert", "shard"), None, None),
    )
    return jax.shard_map(
        shards,
        mesh=mesh,
        in_specs=placed,
        out_specs=(
            P(("expert", "shard"), None, None),
            P(("expert", "shard"), None, None),
            P("shard"),
            P("shard"),
            P("shard", None),
            P("shard", None),
            P("shard"),
            P("shard"),
            P("shard", None),
            P("shard", "expert", None),
            P("shard", "expert", None),
        ),
        check_vma=False,
    )
```

```python
import functools

import jax
import jax.numpy as jnp
from jax import lax
from jax.experimental import pallas as pl
from jax.experimental.pallas import tpu as pltpu
from jax.sharding import PartitionSpec as P

HEADS = 12
EPSILON = 1e-06
CHUNKS = 2
LANES = 128
MIB = 1024 * 1024
BF16 = jnp.bfloat16
F32 = jnp.float32
NN = (((1,), (0,)), ((), ()))
NT = (((1,), (1,)), ((), ()))
TN = (((0,), (0,)), ((), ()))


def dot(a, b, dims=NN):
    return lax.dot_general(a, b, dims, preferred_element_type=F32)


def whole(shape):
    return pl.BlockSpec(shape, lambda *_: (0,) * len(shape), pipeline_mode=pl.Buffered(1))


def cost(products, moved, powers=0):
    return pl.CostEstimate(flops=2 * products, transcendentals=powers, bytes_accessed=moved)


def call(kernel, grid, in_specs, out_specs, out_shape, scratch, limit, estimate):
    return pl.pallas_call(
        kernel,
        grid=grid,
        in_specs=in_specs,
        out_specs=out_specs,
        out_shape=out_shape,
        scratch_shapes=scratch,
        cost_estimate=estimate,
        compiler_params=pltpu.CompilerParams(
            vmem_limit_bytes=limit * MIB,
            dimension_semantics=("arbitrary",) * len(grid),
        ),
    )


def normal(value):
    centered = value - jnp.mean(value, -1, keepdims=True)
    inverse = lax.rsqrt(jnp.mean(centered * centered, -1, keepdims=True) + EPSILON)
    return centered * inverse, inverse


def norm_back(grad, gain, unit, inverse):
    scaled = grad * gain
    return inverse * (
        scaled
        - jnp.mean(scaled, -1, keepdims=True)
        - unit * jnp.mean(scaled * unit, -1, keepdims=True)
    )


def one_hot(equal):
    return jnp.where(equal, 1.0, 0.0).astype(BF16)


def padded_rows(source, buffer):
    group, length, _ = source.shape
    padded = buffer.shape[0] // group
    buffer[...] = jnp.zeros_like(buffer)
    for image in range(group):
        buffer[image * padded : image * padded + length, :] = source[image].astype(buffer.dtype)
    return buffer[...]


def group_of(images):
    return 2 if images % 2 == 0 else 1


def stacked(tile, lane, heads):
    return jnp.concatenate(
        [jnp.where(lane == head, tile, 0.0) for head in range(heads)], 0
    ).astype(BF16)


def unstacked(rows, lane, heads):
    count = rows.shape[0] // heads
    result = rows[0:count, :]
    for head in range(1, heads):
        result = jnp.where(lane == head, rows[head * count : (head + 1) * count, :], result)
    return result


def send_images_kernel(codes_ref, source_ref, out_ref, rows):
    images, length, _ = source_ref.shape
    padded = rows.shape[0] // images
    step = pl.program_id(0)

    @pl.when(step == 0)
    def _():
        rows[...] = jnp.zeros_like(rows)
        for image in range(images):
            rows[image * padded : image * padded + length, :] = source_ref[image].astype(F32)

    pick_rows(codes_ref, rows[...].astype(BF16), out_ref, step)


def send_rows_kernel(codes_ref, source_ref, out_ref):
    pick_rows(codes_ref, source_ref[...], out_ref, pl.program_id(0))


def pick_rows(codes_ref, rows, out_ref, step):
    count = out_ref.shape[1]
    tokens = rows.shape[0]
    slot = lax.broadcasted_iota(jnp.int32, (count, tokens), 0) + step * count
    hot = one_hot((slot == codes_ref[0:1, :]) | (slot == codes_ref[1:2, :]))
    out_ref[0] = dot(hot, rows).astype(BF16)


def send(source, codes, experts, count, width):
    tokens = codes.shape[1]
    if source.ndim == 3:
        kernel, scratch = send_images_kernel, [pltpu.VMEM((tokens, width), F32)]
    else:
        kernel, scratch = send_rows_kernel, []
    return call(
        kernel,
        (experts,),
        [whole(codes.shape), whole(source.shape)],
        pl.BlockSpec((1, count, width), lambda e: (e, 0, 0)),
        jax.ShapeDtypeStruct((experts, count, width), BF16),
        scratch,
        58,
        cost(experts * count * tokens * width, 2 * (tokens + experts * count) * width),
    )(codes, source)


def gather_rows(codes, arrays):
    total = None
    for chunk, array in enumerate(arrays):
        slot = lax.broadcasted_iota(jnp.int32, (codes.shape[0], array.shape[0]), 1)
        first = codes[:, 2 * chunk : 2 * chunk + 1]
        second = codes[:, 2 * chunk + 1 : 2 * chunk + 2]
        part = dot(one_hot((slot == first) | (slot == second)), array[...])
        total = part if total is None else total + part
    return total


def attend_kernel(
    tokens_ref, qkv_weight_ref, out_weight_ref, vector_ref,
    qkv_ref, mixed_ref, attended_ref, first_ref, second_ref, buffer,
):
    group, length, width = tokens_ref.shape
    padded = buffer.shape[0] // group
    value = padded_rows(tokens_ref, buffer)
    unit, _ = normal(value)
    first = (unit * vector_ref[0:1, :] + vector_ref[1:2, :]).astype(BF16)
    first_ref[...] = first.reshape(group, padded, width)
    qkv = dot(first, qkv_weight_ref[...]).astype(BF16)
    qkv_ref[...] = qkv.reshape(group, padded, 3 * width)
    scale = (width // HEADS) ** (-0.5)
    heads = LANES * HEADS // width
    lane = lax.broadcasted_iota(jnp.int32, (padded, LANES), 1) // (width // HEADS)
    real = lax.broadcasted_iota(jnp.int32, (heads * padded, padded), 1) < length
    for image in range(group):
        for at in range(0, width, LANES):
            query = qkv_ref[image, :, at : at + LANES].astype(F32) * scale
            keys = qkv_ref[image, :, width + at : width + at + LANES]
            values = qkv_ref[image, :, 2 * width + at : 2 * width + at + LANES]
            scores = jnp.where(real, dot(stacked(query, lane, heads), keys, NT), -1e30)
            raised = jnp.exp(scores - jnp.max(scores, -1, keepdims=True))
            probs = raised * (1.0 / jnp.sum(raised, -1, keepdims=True))
            result = unstacked(dot(probs.astype(BF16), values), lane, heads)
            mixed_ref[image, :, at : at + LANES] = result.astype(BF16)
    mixed = mixed_ref[...].reshape(group * padded, width)
    attended = buffer[...] + dot(mixed, out_weight_ref[...])
    attended_ref[...] = attended.reshape(group, padded, width)
    unit, _ = normal(attended)
    second = (unit * vector_ref[2:3, :] + vector_ref[3:4, :]).astype(BF16)
    second_ref[...] = second.reshape(group, padded, width)


def attend(tokens, weights, vectors, padded):
    images, length, width = tokens.shape
    group = group_of(images)
    rows = images * padded
    image = lambda cols: pl.BlockSpec((group, padded, cols), lambda i: (i, 0, 0))
    shape = lambda cols, kind: jax.ShapeDtypeStruct((images, padded, cols), kind)
    return call(
        attend_kernel,
        (images // group,),
        [
            pl.BlockSpec((group, length, width), lambda i: (i, 0, 0)),
            pl.BlockSpec((width, 3 * width), lambda i: (0, 0), pipeline_mode=pl.Buffered(1)),
            pl.BlockSpec((width, width), lambda i: (0, 3), pipeline_mode=pl.Buffered(1)),
            whole(vectors.shape),
        ],
        [image(3 * width), image(width), image(width), image(width), image(width)],
        [
            shape(3 * width, BF16), shape(width, BF16), shape(width, F32),
            shape(width, BF16), shape(width, BF16),
        ],
        [pltpu.VMEM((group * padded, width), F32)],
        44,
        cost(
            rows * width * (4 * width + 4 * padded),
            rows * width * 18 + width * width * 8,
            rows * padded * HEADS,
        ),
    )(tokens, weights, weights, vectors)


def gelu_pair(value):
    root = 0.7978845608028654
    cubic = 0.044715
    square = value * value
    bent = jnp.tanh(value * (root + root * cubic * square))
    half = 0.5 + 0.5 * bent
    active = value * half
    slope = half + active * (1.0 - half) * (2.0 * root + 6.0 * root * cubic * square)
    return active, slope


def expert_kernel(experts, block, kept, mine_ref, x_ref, g_ref, up_ref, down_ref, router_ref, *refs):
    (
        out_ref, active_ref, before_ref, scaled_ref, logit_ref, back_ref,
        out_sum, back_sum, probs_ref, x_all_ref,
    ) = refs[kept:]
    step = pl.program_id(0)
    sources, count, width = x_ref.shape
    total = sources * count
    blocks = total // block
    mine = mine_ref[0:1, :]

    @pl.when(step == 0)
    def _():
        out_sum[...] = jnp.zeros_like(out_sum)
        back_sum[...] = jnp.zeros_like(back_sum)
        for source in range(sources):
            rows = slice(source * count, (source + 1) * count)
            x = x_ref[source]
            x_all_ref[rows, :] = x
            logits = dot(x, router_ref[...])
            column = lax.broadcasted_iota(jnp.int32, logits.shape, 1)
            logits = jnp.where(column < experts, logits, -1e30)
            raised = jnp.exp(logits - jnp.max(logits, -1, keepdims=True))
            probs = raised / jnp.sum(raised, -1, keepdims=True)
            probs_ref[rows, :] = probs
            gate = jnp.sum(probs * mine, -1, keepdims=True)
            scaled_ref[rows, :] = (gate * g_ref[source].astype(F32)).astype(BF16)

    def first_products(index):
        rows = slice(index * block, (index + 1) * block)
        before = dot(x_all_ref[rows, :], up_ref[...], NT)
        return before, dot(scaled_ref[rows, :], down_ref[...], NT)

    ahead = first_products(0)
    for index in range(blocks):
        rows = slice(index * block, (index + 1) * block)
        before, active_grad = ahead
        if index + 1 < blocks:
            ahead = first_products(index + 1)
        active, slope = gelu_pair(before)
        active = active.astype(BF16)
        before_grad = (active_grad * slope).astype(BF16)
        active_ref[rows, :] = active
        before_ref[rows, :] = before_grad
        out_sum[rows, :] += dot(active, down_ref[...])
        back_sum[rows, :] += dot(before_grad, up_ref[...])

    @pl.when(step == pl.num_programs(0) - 1)
    def _():
        for source in range(sources):
            rows = slice(source * count, (source + 1) * count)
            made = out_sum[rows, :].astype(BF16).astype(F32)
            probs = probs_ref[rows, :]
            gate = jnp.sum(probs * mine, -1, keepdims=True)
            gate_grad = jnp.sum(made * g_ref[source].astype(F32), -1, keepdims=True)
            logit = (gate_grad * gate * (mine - probs)).astype(BF16)
            logit_ref[rows, :] = logit
            out_ref[source] = (gate * made).astype(BF16)
            back_ref[source] = (
                back_sum[rows, :] + dot(logit, router_ref[...], NT)
            ).astype(BF16)


def run_expert(chunk, kept, mine, x, g, up, down, weights, experts):
    sources, count, width = x.shape
    rows = sources * count
    hidden = up.shape[0]
    part = 768
    block = 256
    last = weights.shape[1] // LANES - 1
    chunk_rows = (sources, count, width)
    wide = pl.BlockSpec((rows, part), lambda f: (0, f))
    weight = pl.BlockSpec((part, width), lambda f: (f, 0))
    slots = pl.BlockSpec(chunk_rows, lambda f: (0, chunk, 0), pipeline_mode=pl.Buffered(1))
    made = lambda cols: jax.ShapeDtypeStruct((rows, cols), BF16)
    return pl.pallas_call(
        functools.partial(expert_kernel, experts, block, len(kept)),
        grid=(hidden // part,),
        in_specs=[
            whole(mine.shape),
            whole(chunk_rows),
            slots,
            weight,
            weight,
            pl.BlockSpec((width, LANES), lambda f: (0, last), pipeline_mode=pl.Buffered(1)),
        ]
        + [pl.BlockSpec(memory_space=pl.ANY)] * len(kept),
        out_specs=[
            slots, wide, wide, whole((rows, width)), whole((rows, LANES)), whole(chunk_rows)
        ],
        out_shape=[
            jax.ShapeDtypeStruct(g.shape, BF16), made(hidden), made(hidden), made(width), made(LANES),
            jax.ShapeDtypeStruct(chunk_rows, BF16),
        ],
        scratch_shapes=[
            pltpu.VMEM((rows, width), F32), pltpu.VMEM((rows, width), F32),
            pltpu.VMEM((rows, LANES), F32), pltpu.VMEM((rows, width), BF16),
        ],
        cost_estimate=cost(4 * rows * width * hidden, 8 * rows * hidden, rows * hidden),
        input_output_aliases={6 + index: index for index in range(len(kept))},
        compiler_params=pltpu.CompilerParams(
            vmem_limit_bytes=56 * MIB, dimension_semantics=("arbitrary",)
        ),
    )(mine, x, g, up, down, weights, *kept)


def attend_back_kernel(*refs):
    codes_ref, *refs = refs
    returned, refs = refs[:CHUNKS], refs[CHUNKS:]
    (
        cotangent_ref, tokens_ref, attended_ref, qkv_ref,
        qkv_weight_ref, out_weight_ref, vector_ref,
        tokens_grad_ref, branch_ref, rows_grad_ref, sums_ref, buffer, mixed_grad_ref,
    ) = refs
    group, length, width = tokens_ref.shape
    padded = buffer.shape[0] // group

    @pl.when(pl.program_id(0) == 0)
    def _():
        sums_ref[...] = jnp.zeros_like(sums_ref)

    codes = codes_ref[...].reshape(group * padded, codes_ref.shape[2])
    second_grad = gather_rows(codes, returned)
    unit, inverse = normal(attended_ref[...].reshape(group * padded, width))
    sums_ref[2:3, :] += jnp.sum(second_grad * unit, 0, keepdims=True)
    sums_ref[3:4, :] += jnp.sum(second_grad, 0, keepdims=True)
    attended_grad = padded_rows(cotangent_ref, buffer) + norm_back(
        second_grad, vector_ref[2:3, :], unit, inverse
    )
    buffer[...] = attended_grad
    branch = attended_grad.astype(BF16)
    branch_ref[...] = branch.reshape(group, padded, width)
    mixed_grad_ref[...] = (
        dot(branch, out_weight_ref[...], NT).astype(BF16).reshape(group, padded, width)
    )
    scale = (width // HEADS) ** (-0.5)
    heads = LANES * HEADS // width
    lane = lax.broadcasted_iota(jnp.int32, (padded, LANES), 1) // (width // HEADS)
    real = lax.broadcasted_iota(jnp.int32, (padded, heads * padded), 0) < length
    for image in range(group):
        for at in range(0, width, LANES):
            query = qkv_ref[image, :, at : at + LANES].astype(F32) * scale
            keys = qkv_ref[image, :, width + at : width + at + LANES]
            values = qkv_ref[image, :, 2 * width + at : 2 * width + at + LANES]
            result = mixed_grad_ref[image, :, at : at + LANES].astype(F32)
            queries = stacked(query, lane, heads)
            results = stacked(result, lane, heads)
            scores = jnp.where(real, dot(keys, queries, NT), -1e30)
            prob_grad = dot(values, results, NT)
            raised = jnp.exp(scores - jnp.max(scores, 0, keepdims=True))
            probs = raised * (1.0 / jnp.sum(raised, 0, keepdims=True))
            score_grad = (
                probs * (prob_grad - jnp.sum(probs * prob_grad, 0, keepdims=True))
            ).astype(BF16)
            keys_scaled = (keys.astype(F32) * scale).astype(BF16)
            grads = (
                unstacked(dot(score_grad, keys_scaled, TN), lane, heads),
                dot(score_grad, queries),
                dot(probs.astype(BF16), results),
            )
            for index, grad in enumerate(grads):
                start = index * width + at
                rows_grad_ref[image, :, start : start + LANES] = grad.astype(BF16)
    rows_grad = rows_grad_ref[...].reshape(group * padded, 3 * width)
    first_grad = dot(rows_grad, qkv_weight_ref[...], NT)
    attended_grad = buffer[...]
    unit, inverse = normal(padded_rows(tokens_ref, buffer))
    sums_ref[0:1, :] += jnp.sum(first_grad * unit, 0, keepdims=True)
    sums_ref[1:2, :] += jnp.sum(first_grad, 0, keepdims=True)
    tokens_grad = attended_grad + norm_back(first_grad, vector_ref[0:1, :], unit, inverse)
    for image in range(group):
        tokens_grad_ref[image] = tokens_grad[
            image * padded : image * padded + length, :
        ].astype(BF16)


def attend_back(codes, returned, cotangent, tokens, attended, qkv, weights, vectors):
    images, length, width = tokens.shape
    padded = attended.shape[1]
    group = group_of(images)
    rows = images * padded
    image = lambda count, cols: pl.BlockSpec((group, count, cols), lambda i: (i, 0, 0))
    return call(
        attend_back_kernel,
        (images // group,),
        [image(padded, codes.shape[2])]
        + [whole(array.shape) for array in returned]
        + [
            image(length, width), image(length, width), image(padded, width), image(padded, 3 * width),
            pl.BlockSpec((width, 3 * width), lambda i: (0, 0), pipeline_mode=pl.Buffered(1)),
            pl.BlockSpec((width, width), lambda i: (0, 3), pipeline_mode=pl.Buffered(1)),
            whole(vectors.shape),
        ],
        [image(length, width), image(padded, width), image(padded, 3 * width), whole((8, width))],
        [
            jax.ShapeDtypeStruct((images, length, width), BF16),
            jax.ShapeDtypeStruct((images, padded, width), BF16),
            jax.ShapeDtypeStruct((images, padded, 3 * width), BF16),
            jax.ShapeDtypeStruct((8, width), F32),
        ],
        [pltpu.VMEM((group * padded, width), F32), pltpu.VMEM((group, padded, width), BF16)],
        56,
        cost(
            rows * width * (4 * width + 10 * padded + CHUNKS * returned[0].shape[0]),
            rows * width * 24 + width * (width * 8 + 4 * returned[0].shape[0]),
            rows * padded * HEADS,
        ),
    )(codes, *returned, cotangent, tokens, attended, qkv, weights, weights, vectors)


def combine_kernel(codes_ref, *refs):
    *returned, attended_ref, out_ref = refs
    group, padded, width = attended_ref.shape
    codes = codes_ref[...].reshape(group * padded, codes_ref.shape[2])
    total = attended_ref[...].reshape(group * padded, width) + gather_rows(codes, returned)
    for image in range(group):
        at = image * padded
        out_ref[image] = total[at : at + out_ref.shape[1], :].astype(BF16)


def combine(codes, returned, attended, length):
    images, padded, width = attended.shape
    group = group_of(images)
    image = lambda rows, cols: pl.BlockSpec((group, rows, cols), lambda i: (i, 0, 0))
    return call(
        combine_kernel,
        (images // group,),
        [image(padded, codes.shape[2])]
        + [whole(array.shape) for array in returned]
        + [image(padded, width)],
        image(length, width),
        jax.ShapeDtypeStruct((images, length, width), BF16),
        [],
        40,
        cost(
            images * padded * width * sum(array.shape[0] for array in returned),
            images * padded * width * 8,
        ),
    )(codes, *returned, attended)


def sum_shards(array):
    size = lax.axis_size("shard")
    rows, cols = array.shape
    pairs = size // 2
    me = lax.axis_index("shard")
    blocks = array.reshape(pairs, 2, rows // size, cols)
    take = lambda core: lax.dynamic_index_in_dim(blocks, core, 1, keepdims=False)
    other = lax.ppermute(take(1 - me % 2), "shard", [(s, s ^ 1) for s in range(size)])
    halves = take(me % 2).astype(F32) + other.astype(F32)
    sent = halves.astype(BF16)
    at = me // 2
    total = lax.dynamic_index_in_dim(halves, at, 0, keepdims=False)
    for shift in range(1, pairs):
        part = lax.dynamic_index_in_dim(sent, (at + shift) % pairs, 0, keepdims=False)
        moves = [(s, (s // 2 + shift) % pairs * 2 + s % 2) for s in range(size)]
        total = total + lax.ppermute(part, "shard", moves).astype(F32)
    return total.astype(BF16)


def sum_experts(array):
    experts = lax.axis_size("expert")
    rows, cols = array.shape
    parts = exchange(array.reshape(experts, rows // experts, cols))
    share = jnp.sum(parts.astype(F32), 0).astype(BF16)
    return lax.all_gather(share, "expert", axis=0, tiled=True).astype(F32)


def exchange(array):
    return lax.all_to_all(array, "expert", split_axis=0, concat_axis=0, tiled=True)


def shards(
    tokens,
    ln1_gain,
    ln1_bias,
    qkv_weight,
    out_weight,
    ln2_gain,
    ln2_bias,
    router_weight,
    up_weight,
    down_weight,
    routes,
    slots,
    keep,
    cotangent,
):
    images, length, width = tokens.shape
    rows = images * length
    experts = lax.axis_size("expert")
    assert up_weight.shape[1] == 1 and router_weight.shape[1] == experts
    capacity = max(4, 5 * rows // (2 * experts))
    count = -(-capacity // (16 * CHUNKS)) * 16
    padded = -(-length // 16) * 16

    routes, slots, keep = (array.transpose(0, 2, 1) for array in (routes, slots, keep))
    fill = ((0, 0), (0, 0), (0, padded - length))
    flat_codes = lambda codes: (
        jnp.pad(codes, fill, constant_values=-1).transpose(1, 0, 2).reshape(2, images * padded)
    )
    all_codes = jnp.where(keep > 0, routes * (CHUNKS * count) + slots, -1)
    g_sent = send(cotangent, flat_codes(all_codes), experts, CHUNKS * count, width)
    g_sent, tokens_in, qkv_weight, routes, slots, keep, all_codes = lax.optimization_barrier(
        (g_sent, tokens, qkv_weight, routes, slots, keep, all_codes)
    )
    g_here = exchange(g_sent)

    columns = experts + 4
    spare = -columns % LANES
    small = jnp.concatenate(
        [router_weight, jnp.stack([ln1_gain, ln1_bias, ln2_gain, ln2_bias], 1)], 1
    )
    packed = jnp.concatenate(
        [qkv_weight, out_weight, jnp.pad(small, ((0, 0), (0, spare)))], 1
    )
    weights = lax.all_gather(packed, "shard", axis=0, tiled=True)
    vectors = jnp.pad(
        weights[:, 4 * width + experts : 4 * width + columns].T.astype(F32), ((0, 4), (0, 0))
    )

    chunk_codes = []
    for chunk in range(CHUNKS):
        place = slots - chunk * count
        here = (keep > 0) & (place >= 0) & (place < count)
        chunk_codes.append(jnp.where(here, routes * count + place, -1))
    row_codes = [flat_codes(codes) for codes in chunk_codes]
    column_codes = lambda codes: jnp.pad(codes, fill, constant_values=-1).transpose(0, 2, 1)
    codes = column_codes(jnp.concatenate(chunk_codes, 1))
    all_codes = column_codes(all_codes)

    up = lax.all_gather(up_weight.reshape(-1, width), "shard", axis=0, tiled=True)
    down = lax.all_gather(down_weight.reshape(-1, width), "shard", axis=0, tiled=True)

    qkv, mixed, attended, first, second = attend(tokens_in, weights, vectors, padded)
    flat_second = second.reshape(images * padded, width)
    mine = (
        lax.broadcasted_iota(jnp.int32, (8, LANES), 1) == lax.axis_index("expert")
    ).astype(F32)

    back_here, wide, kept = [], [], []
    for chunk in range(CHUNKS):
        x = exchange(send(flat_second, row_codes[chunk], experts, count, width))
        out_here, *made, back = run_expert(
            chunk, kept, mine, x, g_here, up, down, weights, experts
        )
        kept = [out_here]
        wide.append((*made, x.reshape(experts * count, width)))
        back_here.append(back)
    wide, back_here[-1] = lax.optimization_barrier((wide, back_here[-1]))

    returned = [exchange(array).reshape(experts * count, width) for array in back_here]
    out_here, returned = lax.optimization_barrier((out_here, returned))
    out_returned = exchange(out_here).reshape(experts * CHUNKS * count, width)

    down_full = sum(dot(active, scaled, TN) for active, _, scaled, _, _ in wide).astype(BF16)
    up_full = sum(dot(before, x, TN) for _, before, _, _, x in wide).astype(BF16)
    router_full = sum(dot(x, logit, TN) for _, _, _, logit, x in wide)
    down_grad = lax.psum_scatter(down_full, "shard", scatter_dimension=0, tiled=True)
    up_grad = lax.psum_scatter(up_full, "shard", scatter_dimension=0, tiled=True)
    _, _, router_full, returned = lax.optimization_barrier(
        (down_full, up_full, router_full, returned)
    )

    tokens_grad, branch, rows_grad, sums = attend_back(
        codes, returned, cotangent, tokens, attended, qkv, weights, vectors
    )
    rows_grad, down_grad, up_grad = lax.optimization_barrier((rows_grad, down_grad, up_grad))
    flat = lambda array: array.reshape(images * padded, -1)
    qkv_full = dot(flat(first), flat(rows_grad), TN)
    out_full = dot(flat(mixed), flat(branch), TN)
    small_full = jnp.concatenate([router_full[:, :experts], sums[0:4].T], 1)
    layer = jnp.concatenate(
        [qkv_full, out_full, jnp.pad(small_full, ((0, 0), (0, spare)))], 1
    ).astype(BF16)
    layer = sum_shards(layer)
    layer, out_returned = lax.optimization_barrier((layer, out_returned))
    layer = sum_experts(layer)
    block_out = combine(all_codes, [out_returned], attended, length)
    tail = 4 * width + experts
    return (
        block_out,
        tokens_grad,
        layer[:, tail],
        layer[:, tail + 1],
        layer[:, : 3 * width],
        layer[:, 3 * width : 4 * width],
        layer[:, tail + 2],
        layer[:, tail + 3],
        layer[:, 4 * width : tail],
        up_grad.astype(F32)[:, None, :],
        down_grad.astype(F32)[:, None, :],
    )


def solution(mesh):
    placed = (
        P(("expert", "shard"), None, None),
        P("shard"),
        P("shard"),
        P("shard", None),
        P("shard", None),
        P("shard"),
        P("shard"),
        P("shard", None),
        P("shard", "expert", None),
        P("shard", "expert", None),
        P(("expert", "shard"), None, None),
        P(("expert", "shard"), None, None),
        P(("expert", "shard"), None, None),
        P(("expert", "shard"), None, None),
    )
    return jax.shard_map(
        shards,
        mesh=mesh,
        in_specs=placed,
        out_specs=(
            P(("expert", "shard"), None, None),
            P(("expert", "shard"), None, None),
            P("shard"),
            P("shard"),
            P("shard", None),
            P("shard", None),
            P("shard"),
            P("shard"),
            P("shard", None),
            P("shard", "expert", None),
            P("shard", "expert", None),
        ),
        check_vma=False,
    )
```

```python
import functools

import jax
import jax.numpy as jnp
from jax import lax
from jax.experimental import pallas as pl
from jax.experimental.pallas import tpu as pltpu
from jax.sharding import PartitionSpec as P

HEADS = 12
EPSILON = 1e-06
CHUNKS = 2
LANES = 128
MIB = 1024 * 1024
BF16 = jnp.bfloat16
F32 = jnp.float32
NN = (((1,), (0,)), ((), ()))
NT = (((1,), (1,)), ((), ()))
TN = (((0,), (0,)), ((), ()))


def dot(a, b, dims=NN):
    return lax.dot_general(a, b, dims, preferred_element_type=F32)


def whole(shape):
    return pl.BlockSpec(shape, lambda *_: (0,) * len(shape), pipeline_mode=pl.Buffered(1))


def cost(products, moved, powers=0):
    return pl.CostEstimate(flops=2 * products, transcendentals=powers, bytes_accessed=moved)


def call(kernel, grid, in_specs, out_specs, out_shape, scratch, limit, estimate):
    return pl.pallas_call(
        kernel,
        grid=grid,
        in_specs=in_specs,
        out_specs=out_specs,
        out_shape=out_shape,
        scratch_shapes=scratch,
        cost_estimate=estimate,
        compiler_params=pltpu.CompilerParams(
            vmem_limit_bytes=limit * MIB,
            dimension_semantics=("arbitrary",) * len(grid),
        ),
    )


def normal(value):
    centered = value - jnp.mean(value, -1, keepdims=True)
    inverse = lax.rsqrt(jnp.mean(centered * centered, -1, keepdims=True) + EPSILON)
    return centered * inverse, inverse


def norm_back(grad, gain, unit, inverse):
    scaled = grad * gain
    return inverse * (
        scaled
        - jnp.mean(scaled, -1, keepdims=True)
        - unit * jnp.mean(scaled * unit, -1, keepdims=True)
    )


def one_hot(equal):
    return jnp.where(equal, 1.0, 0.0).astype(BF16)


def padded_rows(source, buffer):
    group, length, _ = source.shape
    padded = buffer.shape[0] // group
    buffer[...] = jnp.zeros_like(buffer)
    for image in range(group):
        buffer[image * padded : image * padded + length, :] = source[image].astype(buffer.dtype)
    return buffer[...]


def group_of(images):
    return 2 if images % 2 == 0 else 1


def stacked(tile, lane, heads):
    return jnp.concatenate(
        [jnp.where(lane == head, tile, 0.0) for head in range(heads)], 0
    ).astype(BF16)


def unstacked(rows, lane, heads):
    count = rows.shape[0] // heads
    result = rows[0:count, :]
    for head in range(1, heads):
        result = jnp.where(lane == head, rows[head * count : (head + 1) * count, :], result)
    return result


def send_images_kernel(codes_ref, source_ref, out_ref, rows):
    images, length, _ = source_ref.shape
    padded = rows.shape[0] // images
    step = pl.program_id(0)

    @pl.when(step == 0)
    def _():
        rows[...] = jnp.zeros_like(rows)
        for image in range(images):
            rows[image * padded : image * padded + length, :] = source_ref[image].astype(F32)

    pick_rows(codes_ref, rows[...].astype(BF16), out_ref, step)


def send_rows_kernel(codes_ref, source_ref, out_ref):
    pick_rows(codes_ref, source_ref[...], out_ref, pl.program_id(0))


def pick_rows(codes_ref, rows, out_ref, step):
    count = out_ref.shape[1]
    tokens = rows.shape[0]
    slot = lax.broadcasted_iota(jnp.int32, (count, tokens), 0) + step * count
    hot = one_hot((slot == codes_ref[0:1, :]) | (slot == codes_ref[1:2, :]))
    out_ref[0] = dot(hot, rows).astype(BF16)


def send(source, codes, experts, count, width):
    tokens = codes.shape[1]
    if source.ndim == 3:
        kernel, scratch = send_images_kernel, [pltpu.VMEM((tokens, width), F32)]
    else:
        kernel, scratch = send_rows_kernel, []
    return call(
        kernel,
        (experts,),
        [whole(codes.shape), whole(source.shape)],
        pl.BlockSpec((1, count, width), lambda e: (e, 0, 0)),
        jax.ShapeDtypeStruct((experts, count, width), BF16),
        scratch,
        58,
        cost(experts * count * tokens * width, 2 * (tokens + experts * count) * width),
    )(codes, source)


def gather_rows(codes, arrays):
    total = None
    for chunk, array in enumerate(arrays):
        slot = lax.broadcasted_iota(jnp.int32, (codes.shape[0], array.shape[0]), 1)
        first = codes[:, 2 * chunk : 2 * chunk + 1]
        second = codes[:, 2 * chunk + 1 : 2 * chunk + 2]
        part = dot(one_hot((slot == first) | (slot == second)), array[...])
        total = part if total is None else total + part
    return total


def attend_kernel(
    tokens_ref, qkv_weight_ref, out_weight_ref, vector_ref,
    qkv_ref, mixed_ref, attended_ref, first_ref, second_ref, buffer,
):
    group, length, width = tokens_ref.shape
    padded = buffer.shape[0] // group
    value = padded_rows(tokens_ref, buffer)
    unit, _ = normal(value)
    first = (unit * vector_ref[0:1, :] + vector_ref[1:2, :]).astype(BF16)
    first_ref[...] = first.reshape(group, padded, width)
    qkv = dot(first, qkv_weight_ref[...]).astype(BF16)
    qkv_ref[...] = qkv.reshape(group, padded, 3 * width)
    scale = (width // HEADS) ** (-0.5)
    heads = LANES * HEADS // width
    lane = lax.broadcasted_iota(jnp.int32, (padded, LANES), 1) // (width // HEADS)
    real = lax.broadcasted_iota(jnp.int32, (heads * padded, padded), 1) < length
    for image in range(group):
        for at in range(0, width, LANES):
            query = qkv_ref[image, :, at : at + LANES].astype(F32) * scale
            keys = qkv_ref[image, :, width + at : width + at + LANES]
            values = qkv_ref[image, :, 2 * width + at : 2 * width + at + LANES]
            scores = jnp.where(real, dot(stacked(query, lane, heads), keys, NT), -1e30)
            raised = jnp.exp(scores - jnp.max(scores, -1, keepdims=True))
            probs = raised * (1.0 / jnp.sum(raised, -1, keepdims=True))
            result = unstacked(dot(probs.astype(BF16), values), lane, heads)
            mixed_ref[image, :, at : at + LANES] = result.astype(BF16)
    mixed = mixed_ref[...].reshape(group * padded, width)
    attended = buffer[...] + dot(mixed, out_weight_ref[...])
    attended_ref[...] = attended.reshape(group, padded, width)
    unit, _ = normal(attended)
    second = (unit * vector_ref[2:3, :] + vector_ref[3:4, :]).astype(BF16)
    second_ref[...] = second.reshape(group, padded, width)


def attend(tokens, weights, vectors, padded):
    images, length, width = tokens.shape
    group = group_of(images)
    rows = images * padded
    image = lambda cols: pl.BlockSpec((group, padded, cols), lambda i: (i, 0, 0))
    shape = lambda cols, kind: jax.ShapeDtypeStruct((images, padded, cols), kind)
    return call(
        attend_kernel,
        (images // group,),
        [
            pl.BlockSpec((group, length, width), lambda i: (i, 0, 0)),
            pl.BlockSpec((width, 3 * width), lambda i: (0, 0), pipeline_mode=pl.Buffered(1)),
            pl.BlockSpec((width, width), lambda i: (0, 3), pipeline_mode=pl.Buffered(1)),
            whole(vectors.shape),
        ],
        [image(3 * width), image(width), image(width), image(width), image(width)],
        [
            shape(3 * width, BF16), shape(width, BF16), shape(width, F32),
            shape(width, BF16), shape(width, BF16),
        ],
        [pltpu.VMEM((group * padded, width), F32)],
        44,
        cost(
            rows * width * (4 * width + 4 * padded),
            rows * width * 18 + width * width * 8,
            rows * padded * HEADS,
        ),
    )(tokens, weights, weights, vectors)


def gelu_pair(value):
    root = 0.7978845608028654
    cubic = 0.044715
    square = value * value
    bent = jnp.tanh(value * (root + root * cubic * square))
    half = 0.5 + 0.5 * bent
    active = value * half
    slope = half + active * (1.0 - half) * (2.0 * root + 6.0 * root * cubic * square)
    return active, slope


def expert_kernel(experts, block, kept, mine_ref, x_ref, g_ref, up_ref, down_ref, router_ref, *refs):
    (
        out_ref, active_ref, before_ref, scaled_ref, logit_ref, back_ref,
        out_sum, back_sum, probs_ref, x_all_ref,
    ) = refs[kept:]
    step = pl.program_id(0)
    sources, count, width = x_ref.shape
    total = sources * count
    blocks = total // block
    mine = mine_ref[0:1, :]

    @pl.when(step == 0)
    def _():
        out_sum[...] = jnp.zeros_like(out_sum)
        back_sum[...] = jnp.zeros_like(back_sum)
        for source in range(sources):
            rows = slice(source * count, (source + 1) * count)
            x = x_ref[source]
            x_all_ref[rows, :] = x
            logits = dot(x, router_ref[...])
            column = lax.broadcasted_iota(jnp.int32, logits.shape, 1)
            logits = jnp.where(column < experts, logits, -1e30)
            raised = jnp.exp(logits - jnp.max(logits, -1, keepdims=True))
            probs = raised / jnp.sum(raised, -1, keepdims=True)
            probs_ref[rows, :] = probs
            gate = jnp.sum(probs * mine, -1, keepdims=True)
            scaled_ref[rows, :] = (gate * g_ref[source].astype(F32)).astype(BF16)

    def first_products(index):
        rows = slice(index * block, (index + 1) * block)
        before = dot(x_all_ref[rows, :], up_ref[...], NT)
        return before, dot(scaled_ref[rows, :], down_ref[...], NT)

    ahead = first_products(0)
    for index in range(blocks):
        rows = slice(index * block, (index + 1) * block)
        before, active_grad = ahead
        if index + 1 < blocks:
            ahead = first_products(index + 1)
        active, slope = gelu_pair(before)
        active = active.astype(BF16)
        before_grad = (active_grad * slope).astype(BF16)
        active_ref[rows, :] = active
        before_ref[rows, :] = before_grad
        out_sum[rows, :] += dot(active, down_ref[...])
        back_sum[rows, :] += dot(before_grad, up_ref[...])

    @pl.when(step == pl.num_programs(0) - 1)
    def _():
        for source in range(sources):
            rows = slice(source * count, (source + 1) * count)
            made = out_sum[rows, :].astype(BF16).astype(F32)
            probs = probs_ref[rows, :]
            gate = jnp.sum(probs * mine, -1, keepdims=True)
            gate_grad = jnp.sum(made * g_ref[source].astype(F32), -1, keepdims=True)
            logit = (gate_grad * gate * (mine - probs)).astype(BF16)
            logit_ref[rows, :] = logit
            out_ref[source] = (gate * made).astype(BF16)
            back_ref[source] = (
                back_sum[rows, :] + dot(logit, router_ref[...], NT)
            ).astype(BF16)


def run_expert(chunk, kept, mine, x, g, up, down, weights, experts):
    sources, count, width = x.shape
    rows = sources * count
    hidden = up.shape[0]
    part = 768
    block = 256
    last = weights.shape[1] // LANES - 1
    chunk_rows = (sources, count, width)
    wide = pl.BlockSpec((rows, part), lambda f: (0, f))
    weight = pl.BlockSpec((part, width), lambda f: (f, 0))
    slots = pl.BlockSpec(chunk_rows, lambda f: (0, chunk, 0), pipeline_mode=pl.Buffered(1))
    made = lambda cols: jax.ShapeDtypeStruct((rows, cols), BF16)
    return pl.pallas_call(
        functools.partial(expert_kernel, experts, block, len(kept)),
        grid=(hidden // part,),
        in_specs=[
            whole(mine.shape),
            whole(chunk_rows),
            slots,
            weight,
            weight,
            pl.BlockSpec((width, LANES), lambda f: (0, last), pipeline_mode=pl.Buffered(1)),
        ]
        + [pl.BlockSpec(memory_space=pl.ANY)] * len(kept),
        out_specs=[
            slots, wide, wide, whole((rows, width)), whole((rows, LANES)), whole(chunk_rows)
        ],
        out_shape=[
            jax.ShapeDtypeStruct(g.shape, BF16), made(hidden), made(hidden), made(width), made(LANES),
            jax.ShapeDtypeStruct(chunk_rows, BF16),
        ],
        scratch_shapes=[
            pltpu.VMEM((rows, width), F32), pltpu.VMEM((rows, width), F32),
            pltpu.VMEM((rows, LANES), F32), pltpu.VMEM((rows, width), BF16),
        ],
        cost_estimate=cost(4 * rows * width * hidden, 8 * rows * hidden, rows * hidden),
        input_output_aliases={6 + index: index for index in range(len(kept))},
        compiler_params=pltpu.CompilerParams(
            vmem_limit_bytes=56 * MIB, dimension_semantics=("arbitrary",)
        ),
    )(mine, x, g, up, down, weights, *kept)


def attend_back_kernel(*refs):
    codes_ref, *refs = refs
    returned, refs = refs[:CHUNKS], refs[CHUNKS:]
    (
        cotangent_ref, tokens_ref, attended_ref, qkv_ref,
        qkv_weight_ref, out_weight_ref, vector_ref,
        tokens_grad_ref, branch_ref, rows_grad_ref, sums_ref, buffer, mixed_grad_ref,
    ) = refs
    group, length, width = tokens_ref.shape
    padded = buffer.shape[0] // group

    @pl.when(pl.program_id(0) == 0)
    def _():
        sums_ref[...] = jnp.zeros_like(sums_ref)

    codes = codes_ref[...].reshape(group * padded, codes_ref.shape[2])
    second_grad = gather_rows(codes, returned)
    unit, inverse = normal(attended_ref[...].reshape(group * padded, width))
    sums_ref[2:3, :] += jnp.sum(second_grad * unit, 0, keepdims=True)
    sums_ref[3:4, :] += jnp.sum(second_grad, 0, keepdims=True)
    attended_grad = padded_rows(cotangent_ref, buffer) + norm_back(
        second_grad, vector_ref[2:3, :], unit, inverse
    )
    buffer[...] = attended_grad
    branch = attended_grad.astype(BF16)
    branch_ref[...] = branch.reshape(group, padded, width)
    mixed_grad_ref[...] = (
        dot(branch, out_weight_ref[...], NT).astype(BF16).reshape(group, padded, width)
    )
    scale = (width // HEADS) ** (-0.5)
    heads = LANES * HEADS // width
    lane = lax.broadcasted_iota(jnp.int32, (padded, LANES), 1) // (width // HEADS)
    real = lax.broadcasted_iota(jnp.int32, (padded, heads * padded), 0) < length
    for image in range(group):
        for at in range(0, width, LANES):
            query = qkv_ref[image, :, at : at + LANES].astype(F32) * scale
            keys = qkv_ref[image, :, width + at : width + at + LANES]
            values = qkv_ref[image, :, 2 * width + at : 2 * width + at + LANES]
            result = mixed_grad_ref[image, :, at : at + LANES].astype(F32)
            queries = stacked(query, lane, heads)
            results = stacked(result, lane, heads)
            scores = jnp.where(real, dot(keys, queries, NT), -1e30)
            prob_grad = dot(values, results, NT)
            raised = jnp.exp(scores - jnp.max(scores, 0, keepdims=True))
            probs = raised * (1.0 / jnp.sum(raised, 0, keepdims=True))
            score_grad = (
                probs * (prob_grad - jnp.sum(probs * prob_grad, 0, keepdims=True))
            ).astype(BF16)
            keys_scaled = (keys.astype(F32) * scale).astype(BF16)
            grads = (
                unstacked(dot(score_grad, keys_scaled, TN), lane, heads),
                dot(score_grad, queries),
                dot(probs.astype(BF16), results),
            )
            for index, grad in enumerate(grads):
                start = index * width + at
                rows_grad_ref[image, :, start : start + LANES] = grad.astype(BF16)
    rows_grad = rows_grad_ref[...].reshape(group * padded, 3 * width)
    first_grad = dot(rows_grad, qkv_weight_ref[...], NT)
    attended_grad = buffer[...]
    unit, inverse = normal(padded_rows(tokens_ref, buffer))
    sums_ref[0:1, :] += jnp.sum(first_grad * unit, 0, keepdims=True)
    sums_ref[1:2, :] += jnp.sum(first_grad, 0, keepdims=True)
    tokens_grad = attended_grad + norm_back(first_grad, vector_ref[0:1, :], unit, inverse)
    for image in range(group):
        tokens_grad_ref[image] = tokens_grad[
            image * padded : image * padded + length, :
        ].astype(BF16)


def attend_back(codes, returned, cotangent, tokens, attended, qkv, weights, vectors):
    images, length, width = tokens.shape
    padded = attended.shape[1]
    group = group_of(images)
    rows = images * padded
    image = lambda count, cols: pl.BlockSpec((group, count, cols), lambda i: (i, 0, 0))
    return call(
        attend_back_kernel,
        (images // group,),
        [image(padded, codes.shape[2])]
        + [whole(array.shape) for array in returned]
        + [
            image(length, width), image(length, width), image(padded, width), image(padded, 3 * width),
            pl.BlockSpec((width, 3 * width), lambda i: (0, 0), pipeline_mode=pl.Buffered(1)),
            pl.BlockSpec((width, width), lambda i: (0, 3), pipeline_mode=pl.Buffered(1)),
            whole(vectors.shape),
        ],
        [image(length, width), image(padded, width), image(padded, 3 * width), whole((8, width))],
        [
            jax.ShapeDtypeStruct((images, length, width), BF16),
            jax.ShapeDtypeStruct((images, padded, width), BF16),
            jax.ShapeDtypeStruct((images, padded, 3 * width), BF16),
            jax.ShapeDtypeStruct((8, width), F32),
        ],
        [pltpu.VMEM((group * padded, width), F32), pltpu.VMEM((group, padded, width), BF16)],
        56,
        cost(
            rows * width * (4 * width + 10 * padded + CHUNKS * returned[0].shape[0]),
            rows * width * 24 + width * (width * 8 + 4 * returned[0].shape[0]),
            rows * padded * HEADS,
        ),
    )(codes, *returned, cotangent, tokens, attended, qkv, weights, weights, vectors)


def combine_kernel(codes_ref, *refs):
    *returned, attended_ref, out_ref = refs
    group, padded, width = attended_ref.shape
    codes = codes_ref[...].reshape(group * padded, codes_ref.shape[2])
    total = attended_ref[...].reshape(group * padded, width) + gather_rows(codes, returned)
    for image in range(group):
        at = image * padded
        out_ref[image] = total[at : at + out_ref.shape[1], :].astype(BF16)


def combine(codes, returned, attended, length):
    images, padded, width = attended.shape
    group = group_of(images)
    image = lambda rows, cols: pl.BlockSpec((group, rows, cols), lambda i: (i, 0, 0))
    return call(
        combine_kernel,
        (images // group,),
        [image(padded, codes.shape[2])]
        + [whole(array.shape) for array in returned]
        + [image(padded, width)],
        image(length, width),
        jax.ShapeDtypeStruct((images, length, width), BF16),
        [],
        40,
        cost(
            images * padded * width * sum(array.shape[0] for array in returned),
            images * padded * width * 8,
        ),
    )(codes, *returned, attended)


def sum_shards(array):
    size = lax.axis_size("shard")
    rows, cols = array.shape
    pairs = size // 2
    me = lax.axis_index("shard")
    blocks = array.reshape(pairs, 2, rows // size, cols)
    take = lambda core: lax.dynamic_index_in_dim(blocks, core, 1, keepdims=False)
    other = lax.ppermute(take(1 - me % 2), "shard", [(s, s ^ 1) for s in range(size)])
    halves = take(me % 2).astype(F32) + other.astype(F32)
    sent = halves.astype(BF16)
    at = me // 2
    total = lax.dynamic_index_in_dim(halves, at, 0, keepdims=False)
    for shift in range(1, pairs):
        part = lax.dynamic_index_in_dim(sent, (at + shift) % pairs, 0, keepdims=False)
        moves = [(s, (s // 2 + shift) % pairs * 2 + s % 2) for s in range(size)]
        total = total + lax.ppermute(part, "shard", moves).astype(F32)
    return total.astype(BF16)


def sum_experts(array):
    experts = lax.axis_size("expert")
    rows, cols = array.shape
    parts = exchange(array.reshape(experts, rows // experts, cols))
    share = jnp.sum(parts.astype(F32), 0).astype(BF16)
    shares = exchange(jnp.broadcast_to(share[None], parts.shape))
    return shares.reshape(rows, cols).astype(F32)


def exchange(array):
    return lax.all_to_all(array, "expert", split_axis=0, concat_axis=0, tiled=True)


def shards(
    tokens,
    ln1_gain,
    ln1_bias,
    qkv_weight,
    out_weight,
    ln2_gain,
    ln2_bias,
    router_weight,
    up_weight,
    down_weight,
    routes,
    slots,
    keep,
    cotangent,
):
    images, length, width = tokens.shape
    rows = images * length
    experts = lax.axis_size("expert")
    assert up_weight.shape[1] == 1 and router_weight.shape[1] == experts
    capacity = max(4, 5 * rows // (2 * experts))
    count = -(-capacity // (16 * CHUNKS)) * 16
    padded = -(-length // 16) * 16

    routes, slots, keep = (array.transpose(0, 2, 1) for array in (routes, slots, keep))
    fill = ((0, 0), (0, 0), (0, padded - length))
    flat_codes = lambda codes: (
        jnp.pad(codes, fill, constant_values=-1).transpose(1, 0, 2).reshape(2, images * padded)
    )
    all_codes = jnp.where(keep > 0, routes * (CHUNKS * count) + slots, -1)
    g_sent = send(cotangent, flat_codes(all_codes), experts, CHUNKS * count, width)
    g_sent, tokens_in, qkv_weight, routes, slots, keep, all_codes = lax.optimization_barrier(
        (g_sent, tokens, qkv_weight, routes, slots, keep, all_codes)
    )
    g_here = exchange(g_sent)

    columns = experts + 4
    spare = -columns % LANES
    small = jnp.concatenate(
        [router_weight, jnp.stack([ln1_gain, ln1_bias, ln2_gain, ln2_bias], 1)], 1
    )
    packed = jnp.concatenate(
        [qkv_weight, out_weight, jnp.pad(small, ((0, 0), (0, spare)))], 1
    )
    weights = lax.all_gather(packed, "shard", axis=0, tiled=True)
    vectors = jnp.pad(
        weights[:, 4 * width + experts : 4 * width + columns].T.astype(F32), ((0, 4), (0, 0))
    )

    chunk_codes = []
    for chunk in range(CHUNKS):
        place = slots - chunk * count
        here = (keep > 0) & (place >= 0) & (place < count)
        chunk_codes.append(jnp.where(here, routes * count + place, -1))
    row_codes = [flat_codes(codes) for codes in chunk_codes]
    column_codes = lambda codes: jnp.pad(codes, fill, constant_values=-1).transpose(0, 2, 1)
    codes = column_codes(jnp.concatenate(chunk_codes, 1))
    all_codes = column_codes(all_codes)

    up = lax.all_gather(up_weight.reshape(-1, width), "shard", axis=0, tiled=True)
    down = lax.all_gather(down_weight.reshape(-1, width), "shard", axis=0, tiled=True)

    qkv, mixed, attended, first, second = attend(tokens_in, weights, vectors, padded)
    flat_second = second.reshape(images * padded, width)
    mine = (
        lax.broadcasted_iota(jnp.int32, (8, LANES), 1) == lax.axis_index("expert")
    ).astype(F32)

    back_here, wide, kept = [], [], []
    for chunk in range(CHUNKS):
        x = exchange(send(flat_second, row_codes[chunk], experts, count, width))
        out_here, *made, back = run_expert(
            chunk, kept, mine, x, g_here, up, down, weights, experts
        )
        kept = [out_here]
        wide.append((*made, x.reshape(experts * count, width)))
        back_here.append(back)
    returned = []
    for chunk in range(CHUNKS):
        back = back_here[chunk]
        if chunk:
            back, wide, returned = lax.optimization_barrier((back, wide, returned))
        returned.append(exchange(back).reshape(experts * count, width))
    out_here, returned = lax.optimization_barrier((out_here, returned))
    out_returned = exchange(out_here).reshape(experts * CHUNKS * count, width)

    down_full = sum(dot(active, scaled, TN) for active, _, scaled, _, _ in wide).astype(BF16)
    up_full = sum(dot(before, x, TN) for _, before, _, _, x in wide).astype(BF16)
    router_full = sum(dot(x, logit, TN) for _, _, _, logit, x in wide)
    down_full, up_full, router_full, returned = lax.optimization_barrier(
        (down_full, up_full, router_full, returned)
    )
    down_grad = lax.psum_scatter(down_full, "shard", scatter_dimension=0, tiled=True)

    tokens_grad, branch, rows_grad, sums = attend_back(
        codes, returned, cotangent, tokens, attended, qkv, weights, vectors
    )
    flat = lambda array: array.reshape(images * padded, -1)
    qkv_full = dot(flat(first), flat(rows_grad), TN)
    out_full = dot(flat(mixed), flat(branch), TN)
    small_full = jnp.concatenate([router_full[:, :experts], sums[0:4].T], 1)
    layer = jnp.concatenate(
        [qkv_full, out_full, jnp.pad(small_full, ((0, 0), (0, spare)))], 1
    ).astype(BF16)
    layer = sum_shards(layer)
    layer, up_full = lax.optimization_barrier((layer, up_full))
    up_grad = lax.psum_scatter(up_full, "shard", scatter_dimension=0, tiled=True)
    layer, out_returned = lax.optimization_barrier((layer, out_returned))
    layer = sum_experts(layer)
    block_out = combine(all_codes, [out_returned], attended, length)
    tail = 4 * width + experts
    return (
        block_out,
        tokens_grad,
        layer[:, tail],
        layer[:, tail + 1],
        layer[:, : 3 * width],
        layer[:, 3 * width : 4 * width],
        layer[:, tail + 2],
        layer[:, tail + 3],
        layer[:, 4 * width : tail],
        up_grad.astype(F32)[:, None, :],
        down_grad.astype(F32)[:, None, :],
    )


def solution(mesh):
    placed = (
        P(("expert", "shard"), None, None),
        P("shard"),
        P("shard"),
        P("shard", None),
        P("shard", None),
        P("shard"),
        P("shard"),
        P("shard", None),
        P("shard", "expert", None),
        P("shard", "expert", None),
        P(("expert", "shard"), None, None),
        P(("expert", "shard"), None, None),
        P(("expert", "shard"), None, None),
        P(("expert", "shard"), None, None),
    )
    return jax.shard_map(
        shards,
        mesh=mesh,
        in_specs=placed,
        out_specs=(
            P(("expert", "shard"), None, None),
            P(("expert", "shard"), None, None),
            P("shard"),
            P("shard"),
            P("shard", None),
            P("shard", None),
            P("shard"),
            P("shard"),
            P("shard", None),
            P("shard", "expert", None),
            P("shard", "expert", None),
        ),
        check_vma=False,
    )
```

```python
import functools

import jax
import jax.numpy as jnp
from jax import lax
from jax.experimental import pallas as pl
from jax.experimental.pallas import tpu as pltpu
from jax.sharding import PartitionSpec as P

HEADS = 12
EPSILON = 1e-06
CHUNKS = 2
LANES = 128
MIB = 1024 * 1024
BF16 = jnp.bfloat16
F32 = jnp.float32
NN = (((1,), (0,)), ((), ()))
NT = (((1,), (1,)), ((), ()))
TN = (((0,), (0,)), ((), ()))


def dot(a, b, dims=NN):
    return lax.dot_general(a, b, dims, preferred_element_type=F32)


def whole(shape):
    return pl.BlockSpec(shape, lambda *_: (0,) * len(shape), pipeline_mode=pl.Buffered(1))


def cost(products, moved, powers=0):
    return pl.CostEstimate(flops=2 * products, transcendentals=powers, bytes_accessed=moved)


def call(kernel, grid, in_specs, out_specs, out_shape, scratch, limit, estimate):
    return pl.pallas_call(
        kernel,
        grid=grid,
        in_specs=in_specs,
        out_specs=out_specs,
        out_shape=out_shape,
        scratch_shapes=scratch,
        cost_estimate=estimate,
        compiler_params=pltpu.CompilerParams(
            vmem_limit_bytes=limit * MIB,
            dimension_semantics=("arbitrary",) * len(grid),
        ),
    )


def normal(value):
    centered = value - jnp.mean(value, -1, keepdims=True)
    inverse = lax.rsqrt(jnp.mean(centered * centered, -1, keepdims=True) + EPSILON)
    return centered * inverse, inverse


def norm_back(grad, gain, unit, inverse):
    scaled = grad * gain
    return inverse * (
        scaled
        - jnp.mean(scaled, -1, keepdims=True)
        - unit * jnp.mean(scaled * unit, -1, keepdims=True)
    )


def one_hot(equal):
    return jnp.where(equal, 1.0, 0.0).astype(BF16)


def padded_rows(source, buffer):
    group, length, _ = source.shape
    padded = buffer.shape[0] // group
    buffer[...] = jnp.zeros_like(buffer)
    for image in range(group):
        buffer[image * padded : image * padded + length, :] = source[image].astype(buffer.dtype)
    return buffer[...]


def group_of(images):
    return 2 if images % 2 == 0 else 1


def stacked(tile, lane, heads):
    return jnp.concatenate(
        [jnp.where(lane == head, tile, 0.0) for head in range(heads)], 0
    ).astype(BF16)


def unstacked(rows, lane, heads):
    count = rows.shape[0] // heads
    result = rows[0:count, :]
    for head in range(1, heads):
        result = jnp.where(lane == head, rows[head * count : (head + 1) * count, :], result)
    return result


def send_images_kernel(codes_ref, source_ref, out_ref, rows):
    images, length, _ = source_ref.shape
    padded = rows.shape[0] // images
    step = pl.program_id(0)

    @pl.when(step == 0)
    def _():
        rows[...] = jnp.zeros_like(rows)
        for image in range(images):
            rows[image * padded : image * padded + length, :] = source_ref[image].astype(F32)

    pick_rows(codes_ref, rows[...].astype(BF16), out_ref, step)


def send_rows_kernel(codes_ref, source_ref, out_ref):
    pick_rows(codes_ref, source_ref[...], out_ref, pl.program_id(0))


def pick_rows(codes_ref, rows, out_ref, step):
    count = out_ref.shape[1]
    tokens = rows.shape[0]
    slot = lax.broadcasted_iota(jnp.int32, (count, tokens), 0) + step * count
    hot = one_hot((slot == codes_ref[0:1, :]) | (slot == codes_ref[1:2, :]))
    out_ref[0] = dot(hot, rows).astype(BF16)


def send(source, codes, experts, count, width):
    tokens = codes.shape[1]
    if source.ndim == 3:
        kernel, scratch = send_images_kernel, [pltpu.VMEM((tokens, width), F32)]
    else:
        kernel, scratch = send_rows_kernel, []
    return call(
        kernel,
        (experts,),
        [whole(codes.shape), whole(source.shape)],
        pl.BlockSpec((1, count, width), lambda e: (e, 0, 0)),
        jax.ShapeDtypeStruct((experts, count, width), BF16),
        scratch,
        58,
        cost(experts * count * tokens * width, 2 * (tokens + experts * count) * width),
    )(codes, source)


def gather_rows(codes, arrays):
    total = None
    for chunk, array in enumerate(arrays):
        slot = lax.broadcasted_iota(jnp.int32, (codes.shape[0], array.shape[0]), 1)
        first = codes[:, 2 * chunk : 2 * chunk + 1]
        second = codes[:, 2 * chunk + 1 : 2 * chunk + 2]
        part = dot(one_hot((slot == first) | (slot == second)), array[...])
        total = part if total is None else total + part
    return total


def attend_kernel(
    tokens_ref, qkv_weight_ref, out_weight_ref, vector_ref,
    qkv_ref, mixed_ref, attended_ref, first_ref, second_ref, buffer,
):
    group, length, width = tokens_ref.shape
    padded = buffer.shape[0] // group
    value = padded_rows(tokens_ref, buffer)
    unit, _ = normal(value)
    first = (unit * vector_ref[0:1, :] + vector_ref[1:2, :]).astype(BF16)
    first_ref[...] = first.reshape(group, padded, width)
    qkv = dot(first, qkv_weight_ref[...]).astype(BF16)
    qkv_ref[...] = qkv.reshape(group, padded, 3 * width)
    scale = (width // HEADS) ** (-0.5)
    heads = LANES * HEADS // width
    lane = lax.broadcasted_iota(jnp.int32, (padded, LANES), 1) // (width // HEADS)
    real = lax.broadcasted_iota(jnp.int32, (heads * padded, padded), 1) < length
    for image in range(group):
        for at in range(0, width, LANES):
            query = qkv_ref[image, :, at : at + LANES].astype(F32) * scale
            keys = qkv_ref[image, :, width + at : width + at + LANES]
            values = qkv_ref[image, :, 2 * width + at : 2 * width + at + LANES]
            scores = jnp.where(real, dot(stacked(query, lane, heads), keys, NT), -1e30)
            raised = jnp.exp(scores - jnp.max(scores, -1, keepdims=True))
            probs = raised * (1.0 / jnp.sum(raised, -1, keepdims=True))
            result = unstacked(dot(probs.astype(BF16), values), lane, heads)
            mixed_ref[image, :, at : at + LANES] = result.astype(BF16)
    mixed = mixed_ref[...].reshape(group * padded, width)
    attended = buffer[...] + dot(mixed, out_weight_ref[...])
    attended_ref[...] = attended.reshape(group, padded, width)
    unit, _ = normal(attended)
    second = (unit * vector_ref[2:3, :] + vector_ref[3:4, :]).astype(BF16)
    second_ref[...] = second.reshape(group, padded, width)


def attend(tokens, weights, vectors, padded):
    images, length, width = tokens.shape
    group = group_of(images)
    rows = images * padded
    image = lambda cols: pl.BlockSpec((group, padded, cols), lambda i: (i, 0, 0))
    shape = lambda cols, kind: jax.ShapeDtypeStruct((images, padded, cols), kind)
    return call(
        attend_kernel,
        (images // group,),
        [
            pl.BlockSpec((group, length, width), lambda i: (i, 0, 0)),
            pl.BlockSpec((width, 3 * width), lambda i: (0, 0), pipeline_mode=pl.Buffered(1)),
            pl.BlockSpec((width, width), lambda i: (0, 3), pipeline_mode=pl.Buffered(1)),
            whole(vectors.shape),
        ],
        [image(3 * width), image(width), image(width), image(width), image(width)],
        [
            shape(3 * width, BF16), shape(width, BF16), shape(width, F32),
            shape(width, BF16), shape(width, BF16),
        ],
        [pltpu.VMEM((group * padded, width), F32)],
        44,
        cost(
            rows * width * (4 * width + 4 * padded),
            rows * width * 18 + width * width * 8,
            rows * padded * HEADS,
        ),
    )(tokens, weights, weights, vectors)


def gelu_pair(value):
    root = 0.7978845608028654
    cubic = 0.044715
    square = value * value
    bent = jnp.tanh(value * (root + root * cubic * square))
    half = 0.5 + 0.5 * bent
    active = value * half
    slope = half + active * (1.0 - half) * (2.0 * root + 6.0 * root * cubic * square)
    return active, slope


def expert_kernel(
    experts, block, mine_ref, x_ref, g_ref, up_ref, down_ref, router_ref,
    out_ref, active_ref, before_ref, scaled_ref, logit_ref, back_ref,
    out_sum, back_sum, probs_ref, x_all_ref,
):
    step = pl.program_id(0)
    sources, count, width = x_ref.shape
    total = sources * count
    blocks = total // block
    mine = mine_ref[0:1, :]

    @pl.when(step == 0)
    def _():
        out_sum[...] = jnp.zeros_like(out_sum)
        back_sum[...] = jnp.zeros_like(back_sum)
        for source in range(sources):
            rows = slice(source * count, (source + 1) * count)
            x = x_ref[source]
            x_all_ref[rows, :] = x
            logits = dot(x, router_ref[...])
            column = lax.broadcasted_iota(jnp.int32, logits.shape, 1)
            logits = jnp.where(column < experts, logits, -1e30)
            raised = jnp.exp(logits - jnp.max(logits, -1, keepdims=True))
            probs = raised / jnp.sum(raised, -1, keepdims=True)
            probs_ref[rows, :] = probs
            gate = jnp.sum(probs * mine, -1, keepdims=True)
            scaled_ref[rows, :] = (gate * g_ref[source].astype(F32)).astype(BF16)

    def first_products(index):
        rows = slice(index * block, (index + 1) * block)
        before = dot(x_all_ref[rows, :], up_ref[...], NT)
        return before, dot(scaled_ref[rows, :], down_ref[...], NT)

    ahead = first_products(0)
    for index in range(blocks):
        rows = slice(index * block, (index + 1) * block)
        before, active_grad = ahead
        if index + 1 < blocks:
            ahead = first_products(index + 1)
        active, slope = gelu_pair(before)
        active = active.astype(BF16)
        before_grad = (active_grad * slope).astype(BF16)
        active_ref[rows, :] = active
        before_ref[rows, :] = before_grad
        out_sum[rows, :] += dot(active, down_ref[...])
        back_sum[rows, :] += dot(before_grad, up_ref[...])

    @pl.when(step == pl.num_programs(0) - 1)
    def _():
        for source in range(sources):
            rows = slice(source * count, (source + 1) * count)
            made = out_sum[rows, :].astype(BF16).astype(F32)
            probs = probs_ref[rows, :]
            gate = jnp.sum(probs * mine, -1, keepdims=True)
            gate_grad = jnp.sum(made * g_ref[source].astype(F32), -1, keepdims=True)
            logit = (gate_grad * gate * (mine - probs)).astype(BF16)
            logit_ref[rows, :] = logit
            out_ref[source] = (gate * made).astype(BF16)
            back_ref[source] = (
                back_sum[rows, :] + dot(logit, router_ref[...], NT)
            ).astype(BF16)


def run_expert(chunk, mine, x, g, up, down, weights, experts):
    sources, count, width = x.shape
    rows = sources * count
    hidden = up.shape[0]
    part = 768
    block = 256
    last = weights.shape[1] // LANES - 1
    chunk_rows = (sources, count, width)
    wide = pl.BlockSpec((rows, part), lambda f: (0, f))
    weight = pl.BlockSpec((part, width), lambda f: (f, 0))
    slots = pl.BlockSpec(chunk_rows, lambda f: (0, chunk, 0), pipeline_mode=pl.Buffered(1))
    made = lambda cols: jax.ShapeDtypeStruct((rows, cols), BF16)
    return pl.pallas_call(
        functools.partial(expert_kernel, experts, block),
        grid=(hidden // part,),
        in_specs=[
            whole(mine.shape),
            whole(chunk_rows),
            slots,
            weight,
            weight,
            pl.BlockSpec((width, LANES), lambda f: (0, last), pipeline_mode=pl.Buffered(1)),
        ],
        out_specs=[
            whole(chunk_rows), wide, wide, whole((rows, width)), whole((rows, LANES)), whole(chunk_rows)
        ],
        out_shape=[
            jax.ShapeDtypeStruct(chunk_rows, BF16), made(hidden), made(hidden), made(width), made(LANES),
            jax.ShapeDtypeStruct(chunk_rows, BF16),
        ],
        scratch_shapes=[
            pltpu.VMEM((rows, width), F32), pltpu.VMEM((rows, width), F32),
            pltpu.VMEM((rows, LANES), F32), pltpu.VMEM((rows, width), BF16),
        ],
        cost_estimate=cost(4 * rows * width * hidden, 8 * rows * hidden, rows * hidden),
        compiler_params=pltpu.CompilerParams(
            vmem_limit_bytes=56 * MIB, dimension_semantics=("arbitrary",)
        ),
    )(mine, x, g, up, down, weights)


def attend_back_kernel(*refs):
    codes_ref, *refs = refs
    returned, refs = refs[:CHUNKS], refs[CHUNKS:]
    (
        cotangent_ref, tokens_ref, attended_ref, qkv_ref,
        qkv_weight_ref, out_weight_ref, vector_ref,
        tokens_grad_ref, branch_ref, rows_grad_ref, sums_ref, buffer, mixed_grad_ref,
    ) = refs
    group, length, width = tokens_ref.shape
    padded = buffer.shape[0] // group

    @pl.when(pl.program_id(0) == 0)
    def _():
        sums_ref[...] = jnp.zeros_like(sums_ref)

    codes = codes_ref[...].reshape(group * padded, codes_ref.shape[2])
    second_grad = gather_rows(codes, returned)
    unit, inverse = normal(attended_ref[...].reshape(group * padded, width))
    sums_ref[2:3, :] += jnp.sum(second_grad * unit, 0, keepdims=True)
    sums_ref[3:4, :] += jnp.sum(second_grad, 0, keepdims=True)
    attended_grad = padded_rows(cotangent_ref, buffer) + norm_back(
        second_grad, vector_ref[2:3, :], unit, inverse
    )
    buffer[...] = attended_grad
    branch = attended_grad.astype(BF16)
    branch_ref[...] = branch.reshape(group, padded, width)
    mixed_grad_ref[...] = (
        dot(branch, out_weight_ref[...], NT).astype(BF16).reshape(group, padded, width)
    )
    scale = (width // HEADS) ** (-0.5)
    heads = LANES * HEADS // width
    lane = lax.broadcasted_iota(jnp.int32, (padded, LANES), 1) // (width // HEADS)
    real = lax.broadcasted_iota(jnp.int32, (padded, heads * padded), 0) < length
    for image in range(group):
        for at in range(0, width, LANES):
            query = qkv_ref[image, :, at : at + LANES].astype(F32) * scale
            keys = qkv_ref[image, :, width + at : width + at + LANES]
            values = qkv_ref[image, :, 2 * width + at : 2 * width + at + LANES]
            result = mixed_grad_ref[image, :, at : at + LANES].astype(F32)
            queries = stacked(query, lane, heads)
            results = stacked(result, lane, heads)
            scores = jnp.where(real, dot(keys, queries, NT), -1e30)
            prob_grad = dot(values, results, NT)
            raised = jnp.exp(scores - jnp.max(scores, 0, keepdims=True))
            probs = raised * (1.0 / jnp.sum(raised, 0, keepdims=True))
            score_grad = (
                probs * (prob_grad - jnp.sum(probs * prob_grad, 0, keepdims=True))
            ).astype(BF16)
            keys_scaled = (keys.astype(F32) * scale).astype(BF16)
            grads = (
                unstacked(dot(score_grad, keys_scaled, TN), lane, heads),
                dot(score_grad, queries),
                dot(probs.astype(BF16), results),
            )
            for index, grad in enumerate(grads):
                start = index * width + at
                rows_grad_ref[image, :, start : start + LANES] = grad.astype(BF16)
    rows_grad = rows_grad_ref[...].reshape(group * padded, 3 * width)
    first_grad = dot(rows_grad, qkv_weight_ref[...], NT)
    attended_grad = buffer[...]
    unit, inverse = normal(padded_rows(tokens_ref, buffer))
    sums_ref[0:1, :] += jnp.sum(first_grad * unit, 0, keepdims=True)
    sums_ref[1:2, :] += jnp.sum(first_grad, 0, keepdims=True)
    tokens_grad = attended_grad + norm_back(first_grad, vector_ref[0:1, :], unit, inverse)
    for image in range(group):
        tokens_grad_ref[image] = tokens_grad[
            image * padded : image * padded + length, :
        ].astype(BF16)


def attend_back(codes, returned, cotangent, tokens, attended, qkv, weights, vectors):
    images, length, width = tokens.shape
    padded = attended.shape[1]
    group = group_of(images)
    rows = images * padded
    image = lambda count, cols: pl.BlockSpec((group, count, cols), lambda i: (i, 0, 0))
    return call(
        attend_back_kernel,
        (images // group,),
        [image(padded, codes.shape[2])]
        + [whole(array.shape) for array in returned]
        + [
            image(length, width), image(length, width), image(padded, width), image(padded, 3 * width),
            pl.BlockSpec((width, 3 * width), lambda i: (0, 0), pipeline_mode=pl.Buffered(1)),
            pl.BlockSpec((width, width), lambda i: (0, 3), pipeline_mode=pl.Buffered(1)),
            whole(vectors.shape),
        ],
        [image(length, width), image(padded, width), image(padded, 3 * width), whole((8, width))],
        [
            jax.ShapeDtypeStruct((images, length, width), BF16),
            jax.ShapeDtypeStruct((images, padded, width), BF16),
            jax.ShapeDtypeStruct((images, padded, 3 * width), BF16),
            jax.ShapeDtypeStruct((8, width), F32),
        ],
        [pltpu.VMEM((group * padded, width), F32), pltpu.VMEM((group, padded, width), BF16)],
        56,
        cost(
            rows * width * (4 * width + 10 * padded + CHUNKS * returned[0].shape[0]),
            rows * width * 24 + width * (width * 8 + 4 * returned[0].shape[0]),
            rows * padded * HEADS,
        ),
    )(codes, *returned, cotangent, tokens, attended, qkv, weights, weights, vectors)


def combine_kernel(codes_ref, *refs):
    *returned, attended_ref, out_ref = refs
    group, padded, width = attended_ref.shape
    codes = codes_ref[...].reshape(group * padded, codes_ref.shape[2])
    total = attended_ref[...].reshape(group * padded, width) + gather_rows(codes, returned)
    for image in range(group):
        at = image * padded
        out_ref[image] = total[at : at + out_ref.shape[1], :].astype(BF16)


def combine(codes, returned, attended, length):
    images, padded, width = attended.shape
    group = group_of(images)
    image = lambda rows, cols: pl.BlockSpec((group, rows, cols), lambda i: (i, 0, 0))
    return call(
        combine_kernel,
        (images // group,),
        [image(padded, codes.shape[2])]
        + [whole(array.shape) for array in returned]
        + [image(padded, width)],
        image(length, width),
        jax.ShapeDtypeStruct((images, length, width), BF16),
        [],
        40,
        cost(
            images * padded * width * sum(array.shape[0] for array in returned),
            images * padded * width * 8,
        ),
    )(codes, *returned, attended)


def sum_shards(array):
    size = lax.axis_size("shard")
    rows, cols = array.shape
    pairs = size // 2
    me = lax.axis_index("shard")
    blocks = array.reshape(pairs, 2, rows // size, cols)
    take = lambda core: lax.dynamic_index_in_dim(blocks, core, 1, keepdims=False)
    other = lax.ppermute(take(1 - me % 2), "shard", [(s, s ^ 1) for s in range(size)])
    halves = take(me % 2).astype(F32) + other.astype(F32)
    sent = halves.astype(BF16)
    at = me // 2
    total = lax.dynamic_index_in_dim(halves, at, 0, keepdims=False)
    for shift in range(1, pairs):
        part = lax.dynamic_index_in_dim(sent, (at + shift) % pairs, 0, keepdims=False)
        moves = [(s, (s // 2 + shift) % pairs * 2 + s % 2) for s in range(size)]
        total = total + lax.ppermute(part, "shard", moves).astype(F32)
    return total.astype(BF16)


def sum_experts(array):
    experts = lax.axis_size("expert")
    rows, cols = array.shape
    parts = exchange(array.reshape(experts, rows // experts, cols))
    share = jnp.sum(parts.astype(F32), 0).astype(BF16)
    shares = exchange(jnp.broadcast_to(share[None], parts.shape))
    return shares.reshape(rows, cols).astype(F32)


def exchange(array):
    return lax.all_to_all(array, "expert", split_axis=0, concat_axis=0, tiled=True)


def shards(
    tokens,
    ln1_gain,
    ln1_bias,
    qkv_weight,
    out_weight,
    ln2_gain,
    ln2_bias,
    router_weight,
    up_weight,
    down_weight,
    routes,
    slots,
    keep,
    cotangent,
):
    images, length, width = tokens.shape
    rows = images * length
    experts = lax.axis_size("expert")
    assert up_weight.shape[1] == 1 and router_weight.shape[1] == experts
    capacity = max(4, 5 * rows // (2 * experts))
    count = -(-capacity // (16 * CHUNKS)) * 16
    padded = -(-length // 16) * 16

    routes, slots, keep = (array.transpose(0, 2, 1) for array in (routes, slots, keep))
    fill = ((0, 0), (0, 0), (0, padded - length))
    flat_codes = lambda codes: (
        jnp.pad(codes, fill, constant_values=-1).transpose(1, 0, 2).reshape(2, images * padded)
    )
    all_codes = jnp.where(keep > 0, routes * (CHUNKS * count) + slots, -1)
    g_sent = send(cotangent, flat_codes(all_codes), experts, CHUNKS * count, width)
    g_sent, tokens_in, qkv_weight, routes, slots, keep = lax.optimization_barrier(
        (g_sent, tokens, qkv_weight, routes, slots, keep)
    )
    g_here = exchange(g_sent)

    columns = experts + 4
    spare = -columns % LANES
    small = jnp.concatenate(
        [router_weight, jnp.stack([ln1_gain, ln1_bias, ln2_gain, ln2_bias], 1)], 1
    )
    packed = jnp.concatenate(
        [qkv_weight, out_weight, jnp.pad(small, ((0, 0), (0, spare)))], 1
    )
    weights = lax.all_gather(packed, "shard", axis=0, tiled=True)
    vectors = jnp.pad(
        weights[:, 4 * width + experts : 4 * width + columns].T.astype(F32), ((0, 4), (0, 0))
    )

    chunk_codes = []
    for chunk in range(CHUNKS):
        place = slots - chunk * count
        here = (keep > 0) & (place >= 0) & (place < count)
        chunk_codes.append(jnp.where(here, routes * count + place, -1))
    row_codes = [flat_codes(codes) for codes in chunk_codes]
    codes = jnp.pad(
        jnp.concatenate(chunk_codes, 1), fill, constant_values=-1
    ).transpose(0, 2, 1)

    up = lax.all_gather(up_weight.reshape(-1, width), "shard", axis=0, tiled=True)
    down = lax.all_gather(down_weight.reshape(-1, width), "shard", axis=0, tiled=True)

    qkv, mixed, attended, first, second = attend(tokens_in, weights, vectors, padded)
    flat_second = second.reshape(images * padded, width)
    mine = (
        lax.broadcasted_iota(jnp.int32, (8, LANES), 1) == lax.axis_index("expert")
    ).astype(F32)

    back_here, out_here, wide, up_parts = [], [], [], []
    for chunk in range(CHUNKS):
        x = exchange(send(flat_second, row_codes[chunk], experts, count, width))
        if chunk:
            x, up_parts = lax.optimization_barrier((x, up_parts))
        out, *made, back = run_expert(chunk, mine, x, g_here, up, down, weights, experts)
        out_here.append(out)
        back_here.append(back)
        wide.append((*made, x.reshape(experts * count, width)))
        if chunk < CHUNKS - 1:
            up_parts.append(dot(made[1], wide[chunk][4], TN))
    returned = []
    for chunk in range(CHUNKS):
        back = back_here[chunk]
        if chunk:
            back, wide, returned = lax.optimization_barrier((back, wide, returned))
        returned.append(exchange(back).reshape(experts * count, width))
    out_returned = []
    for out in out_here:
        out, returned, out_returned = lax.optimization_barrier((out, returned, out_returned))
        out_returned.append(exchange(out).reshape(experts * count, width))

    down_full = sum(dot(active, scaled, TN) for active, _, scaled, _, _ in wide).astype(BF16)
    _, before, _, _, x = wide[-1]
    up_full = sum(up_parts, dot(before, x, TN)).astype(BF16)
    router_full = sum(dot(x, logit, TN) for _, _, _, logit, x in wide)
    down_full, up_full, router_full, returned = lax.optimization_barrier(
        (down_full, up_full, router_full, returned)
    )
    down_grad = lax.psum_scatter(down_full, "shard", scatter_dimension=0, tiled=True)

    tokens_grad, branch, rows_grad, sums = attend_back(
        codes, returned, cotangent, tokens, attended, qkv, weights, vectors
    )
    flat = lambda array: array.reshape(images * padded, -1)
    qkv_full = dot(flat(first), flat(rows_grad), TN)
    out_full = dot(flat(mixed), flat(branch), TN)
    small_full = jnp.concatenate([router_full[:, :experts], sums[0:4].T], 1)
    layer = jnp.concatenate(
        [qkv_full, out_full, jnp.pad(small_full, ((0, 0), (0, spare)))], 1
    ).astype(BF16)
    layer, out_returned[0] = lax.optimization_barrier((layer, out_returned[0]))
    layer = sum_shards(layer)
    layer, up_full = lax.optimization_barrier((layer, up_full))
    up_grad = lax.psum_scatter(up_full, "shard", scatter_dimension=0, tiled=True)
    layer, out_returned = lax.optimization_barrier((layer, out_returned))
    layer = sum_experts(layer)
    block_out = combine(codes, out_returned, attended, length)
    tail = 4 * width + experts
    return (
        block_out,
        tokens_grad,
        layer[:, tail],
        layer[:, tail + 1],
        layer[:, : 3 * width],
        layer[:, 3 * width : 4 * width],
        layer[:, tail + 2],
        layer[:, tail + 3],
        layer[:, 4 * width : tail],
        up_grad.astype(F32)[:, None, :],
        down_grad.astype(F32)[:, None, :],
    )


def solution(mesh):
    placed = (
        P(("expert", "shard"), None, None),
        P("shard"),
        P("shard"),
        P("shard", None),
        P("shard", None),
        P("shard"),
        P("shard"),
        P("shard", None),
        P("shard", "expert", None),
        P("shard", "expert", None),
        P(("expert", "shard"), None, None),
        P(("expert", "shard"), None, None),
        P(("expert", "shard"), None, None),
        P(("expert", "shard"), None, None),
    )
    return jax.shard_map(
        shards,
        mesh=mesh,
        in_specs=placed,
        out_specs=(
            P(("expert", "shard"), None, None),
            P(("expert", "shard"), None, None),
            P("shard"),
            P("shard"),
            P("shard", None),
            P("shard", None),
            P("shard"),
            P("shard"),
            P("shard", None),
            P("shard", "expert", None),
            P("shard", "expert", None),
        ),
        check_vma=False,
    )
```

```python
import functools

import jax
import jax.numpy as jnp
from jax import lax
from jax.experimental import pallas as pl
from jax.experimental.pallas import tpu as pltpu
from jax.sharding import PartitionSpec as P

HEADS = 12
EPSILON = 1e-06
CHUNKS = 2
LANES = 128
MIB = 1024 * 1024
BF16 = jnp.bfloat16
F32 = jnp.float32
NN = (((1,), (0,)), ((), ()))
NT = (((1,), (1,)), ((), ()))
TN = (((0,), (0,)), ((), ()))


def dot(a, b, dims=NN):
    return lax.dot_general(a, b, dims, preferred_element_type=F32)


def whole(shape):
    return pl.BlockSpec(shape, lambda *_: (0,) * len(shape), pipeline_mode=pl.Buffered(1))


def cost(products, moved, powers=0):
    return pl.CostEstimate(flops=2 * products, transcendentals=powers, bytes_accessed=moved)


def call(kernel, grid, in_specs, out_specs, out_shape, scratch, limit, estimate):
    return pl.pallas_call(
        kernel,
        grid=grid,
        in_specs=in_specs,
        out_specs=out_specs,
        out_shape=out_shape,
        scratch_shapes=scratch,
        cost_estimate=estimate,
        compiler_params=pltpu.CompilerParams(
            vmem_limit_bytes=limit * MIB,
            dimension_semantics=("arbitrary",) * len(grid),
        ),
    )


def normal(value):
    centered = value - jnp.mean(value, -1, keepdims=True)
    inverse = lax.rsqrt(jnp.mean(centered * centered, -1, keepdims=True) + EPSILON)
    return centered * inverse, inverse


def norm_back(grad, gain, unit, inverse):
    scaled = grad * gain
    return inverse * (
        scaled
        - jnp.mean(scaled, -1, keepdims=True)
        - unit * jnp.mean(scaled * unit, -1, keepdims=True)
    )


def one_hot(equal):
    return jnp.where(equal, 1.0, 0.0).astype(BF16)


def padded_rows(source, buffer):
    group, length, _ = source.shape
    padded = buffer.shape[0] // group
    buffer[...] = jnp.zeros_like(buffer)
    for image in range(group):
        buffer[image * padded : image * padded + length, :] = source[image].astype(buffer.dtype)
    return buffer[...]


def group_of(images):
    return 2 if images % 2 == 0 else 1


def stacked(tile, lane, heads):
    return jnp.concatenate(
        [jnp.where(lane == head, tile, 0.0) for head in range(heads)], 0
    ).astype(BF16)


def unstacked(rows, lane, heads):
    count = rows.shape[0] // heads
    result = rows[0:count, :]
    for head in range(1, heads):
        result = jnp.where(lane == head, rows[head * count : (head + 1) * count, :], result)
    return result


def send_images_kernel(codes_ref, source_ref, out_ref, rows):
    images, length, _ = source_ref.shape
    padded = rows.shape[0] // images
    step = pl.program_id(0)

    @pl.when(step == 0)
    def _():
        rows[...] = jnp.zeros_like(rows)
        for image in range(images):
            rows[image * padded : image * padded + length, :] = source_ref[image].astype(F32)

    pick_rows(codes_ref, rows[...].astype(BF16), out_ref, step)


def send_rows_kernel(codes_ref, source_ref, out_ref):
    pick_rows(codes_ref, source_ref[...], out_ref, pl.program_id(0))


def pick_rows(codes_ref, rows, out_ref, step):
    count = out_ref.shape[1]
    tokens = rows.shape[0]
    slot = lax.broadcasted_iota(jnp.int32, (count, tokens), 0) + step * count
    hot = one_hot((slot == codes_ref[0:1, :]) | (slot == codes_ref[1:2, :]))
    out_ref[0] = dot(hot, rows).astype(BF16)


def send(source, codes, experts, count, width):
    tokens = codes.shape[1]
    if source.ndim == 3:
        kernel, scratch = send_images_kernel, [pltpu.VMEM((tokens, width), F32)]
    else:
        kernel, scratch = send_rows_kernel, []
    return call(
        kernel,
        (experts,),
        [whole(codes.shape), whole(source.shape)],
        pl.BlockSpec((1, count, width), lambda e: (e, 0, 0)),
        jax.ShapeDtypeStruct((experts, count, width), BF16),
        scratch,
        58,
        cost(experts * count * tokens * width, 2 * (tokens + experts * count) * width),
    )(codes, source)


def gather_rows(codes, arrays):
    total = None
    for chunk, array in enumerate(arrays):
        slot = lax.broadcasted_iota(jnp.int32, (codes.shape[0], array.shape[0]), 1)
        first = codes[:, 2 * chunk : 2 * chunk + 1]
        second = codes[:, 2 * chunk + 1 : 2 * chunk + 2]
        part = dot(one_hot((slot == first) | (slot == second)), array[...])
        total = part if total is None else total + part
    return total


def attend_kernel(
    tokens_ref, qkv_weight_ref, out_weight_ref, vector_ref,
    qkv_ref, mixed_ref, attended_ref, first_ref, second_ref, buffer,
):
    group, length, width = tokens_ref.shape
    padded = buffer.shape[0] // group
    value = padded_rows(tokens_ref, buffer)
    unit, _ = normal(value)
    first = (unit * vector_ref[0:1, :] + vector_ref[1:2, :]).astype(BF16)
    first_ref[...] = first.reshape(group, padded, width)
    qkv = dot(first, qkv_weight_ref[...]).astype(BF16)
    qkv_ref[...] = qkv.reshape(group, padded, 3 * width)
    scale = (width // HEADS) ** (-0.5)
    heads = LANES * HEADS // width
    lane = lax.broadcasted_iota(jnp.int32, (padded, LANES), 1) // (width // HEADS)
    real = lax.broadcasted_iota(jnp.int32, (heads * padded, padded), 1) < length
    for image in range(group):
        for at in range(0, width, LANES):
            query = qkv_ref[image, :, at : at + LANES].astype(F32) * scale
            keys = qkv_ref[image, :, width + at : width + at + LANES]
            values = qkv_ref[image, :, 2 * width + at : 2 * width + at + LANES]
            scores = jnp.where(real, dot(stacked(query, lane, heads), keys, NT), -1e30)
            raised = jnp.exp(scores - jnp.max(scores, -1, keepdims=True))
            probs = raised * (1.0 / jnp.sum(raised, -1, keepdims=True))
            result = unstacked(dot(probs.astype(BF16), values), lane, heads)
            mixed_ref[image, :, at : at + LANES] = result.astype(BF16)
    mixed = mixed_ref[...].reshape(group * padded, width)
    attended = buffer[...] + dot(mixed, out_weight_ref[...])
    attended_ref[...] = attended.reshape(group, padded, width)
    unit, _ = normal(attended)
    second = (unit * vector_ref[2:3, :] + vector_ref[3:4, :]).astype(BF16)
    second_ref[...] = second.reshape(group, padded, width)


def attend(tokens, weights, vectors, padded):
    images, length, width = tokens.shape
    group = group_of(images)
    rows = images * padded
    image = lambda cols: pl.BlockSpec((group, padded, cols), lambda i: (i, 0, 0))
    shape = lambda cols, kind: jax.ShapeDtypeStruct((images, padded, cols), kind)
    return call(
        attend_kernel,
        (images // group,),
        [
            pl.BlockSpec((group, length, width), lambda i: (i, 0, 0)),
            pl.BlockSpec((width, 3 * width), lambda i: (0, 0), pipeline_mode=pl.Buffered(1)),
            pl.BlockSpec((width, width), lambda i: (0, 3), pipeline_mode=pl.Buffered(1)),
            whole(vectors.shape),
        ],
        [image(3 * width), image(width), image(width), image(width), image(width)],
        [
            shape(3 * width, BF16), shape(width, BF16), shape(width, F32),
            shape(width, BF16), shape(width, BF16),
        ],
        [pltpu.VMEM((group * padded, width), F32)],
        44,
        cost(
            rows * width * (4 * width + 4 * padded),
            rows * width * 18 + width * width * 8,
            rows * padded * HEADS,
        ),
    )(tokens, weights, weights, vectors)


def gelu_pair(value):
    root = 0.7978845608028654
    cubic = 0.044715
    square = value * value
    bent = jnp.tanh(value * (root + root * cubic * square))
    half = 0.5 + 0.5 * bent
    active = value * half
    slope = half + active * (1.0 - half) * (2.0 * root + 6.0 * root * cubic * square)
    return active, slope


def expert_kernel(
    experts, block, mine_ref, x_ref, g_ref, up_ref, down_ref, router_ref,
    out_ref, active_ref, before_ref, scaled_ref, logit_ref, back_ref,
    out_sum, back_sum, probs_ref, x_all_ref,
):
    step = pl.program_id(0)
    sources, count, width = x_ref.shape
    total = sources * count
    blocks = total // block
    mine = mine_ref[0:1, :]

    @pl.when(step == 0)
    def _():
        out_sum[...] = jnp.zeros_like(out_sum)
        back_sum[...] = jnp.zeros_like(back_sum)
        for source in range(sources):
            rows = slice(source * count, (source + 1) * count)
            x = x_ref[source]
            x_all_ref[rows, :] = x
            logits = dot(x, router_ref[...])
            column = lax.broadcasted_iota(jnp.int32, logits.shape, 1)
            logits = jnp.where(column < experts, logits, -1e30)
            raised = jnp.exp(logits - jnp.max(logits, -1, keepdims=True))
            probs = raised / jnp.sum(raised, -1, keepdims=True)
            probs_ref[rows, :] = probs
            gate = jnp.sum(probs * mine, -1, keepdims=True)
            scaled_ref[rows, :] = (gate * g_ref[source].astype(F32)).astype(BF16)

    def first_products(index):
        rows = slice(index * block, (index + 1) * block)
        before = dot(x_all_ref[rows, :], up_ref[...], NT)
        return before, dot(scaled_ref[rows, :], down_ref[...], NT)

    ahead = first_products(0)
    for index in range(blocks):
        rows = slice(index * block, (index + 1) * block)
        before, active_grad = ahead
        if index + 1 < blocks:
            ahead = first_products(index + 1)
        active, slope = gelu_pair(before)
        active = active.astype(BF16)
        before_grad = (active_grad * slope).astype(BF16)
        active_ref[rows, :] = active
        before_ref[rows, :] = before_grad
        out_sum[rows, :] += dot(active, down_ref[...])
        back_sum[rows, :] += dot(before_grad, up_ref[...])

    @pl.when(step == pl.num_programs(0) - 1)
    def _():
        for source in range(sources):
            rows = slice(source * count, (source + 1) * count)
            made = out_sum[rows, :].astype(BF16).astype(F32)
            probs = probs_ref[rows, :]
            gate = jnp.sum(probs * mine, -1, keepdims=True)
            gate_grad = jnp.sum(made * g_ref[source].astype(F32), -1, keepdims=True)
            logit = (gate_grad * gate * (mine - probs)).astype(BF16)
            logit_ref[rows, :] = logit
            out_ref[source] = (gate * made).astype(BF16)
            back_ref[source] = (
                back_sum[rows, :] + dot(logit, router_ref[...], NT)
            ).astype(BF16)


def run_expert(chunk, mine, x, g, up, down, weights, experts):
    sources, count, width = x.shape
    rows = sources * count
    hidden = up.shape[0]
    part = 768
    block = 256
    last = weights.shape[1] // LANES - 1
    chunk_rows = (sources, count, width)
    wide = pl.BlockSpec((rows, part), lambda f: (0, f))
    weight = pl.BlockSpec((part, width), lambda f: (f, 0))
    slots = pl.BlockSpec(chunk_rows, lambda f: (0, chunk, 0), pipeline_mode=pl.Buffered(1))
    made = lambda cols: jax.ShapeDtypeStruct((rows, cols), BF16)
    return pl.pallas_call(
        functools.partial(expert_kernel, experts, block),
        grid=(hidden // part,),
        in_specs=[
            whole(mine.shape),
            whole(chunk_rows),
            slots,
            weight,
            weight,
            pl.BlockSpec((width, LANES), lambda f: (0, last), pipeline_mode=pl.Buffered(1)),
        ],
        out_specs=[
            whole(chunk_rows), wide, wide, whole((rows, width)), whole((rows, LANES)), whole(chunk_rows)
        ],
        out_shape=[
            jax.ShapeDtypeStruct(chunk_rows, BF16), made(hidden), made(hidden), made(width), made(LANES),
            jax.ShapeDtypeStruct(chunk_rows, BF16),
        ],
        scratch_shapes=[
            pltpu.VMEM((rows, width), F32), pltpu.VMEM((rows, width), F32),
            pltpu.VMEM((rows, LANES), F32), pltpu.VMEM((rows, width), BF16),
        ],
        cost_estimate=cost(4 * rows * width * hidden, 8 * rows * hidden, rows * hidden),
        compiler_params=pltpu.CompilerParams(
            vmem_limit_bytes=56 * MIB, dimension_semantics=("arbitrary",)
        ),
    )(mine, x, g, up, down, weights)


def attend_back_kernel(*refs):
    codes_ref, *refs = refs
    returned, refs = refs[:CHUNKS], refs[CHUNKS:]
    (
        cotangent_ref, tokens_ref, attended_ref, qkv_ref,
        qkv_weight_ref, out_weight_ref, vector_ref,
        tokens_grad_ref, branch_ref, rows_grad_ref, sums_ref, buffer, mixed_grad_ref,
    ) = refs
    group, length, width = tokens_ref.shape
    padded = buffer.shape[0] // group

    @pl.when(pl.program_id(0) == 0)
    def _():
        sums_ref[...] = jnp.zeros_like(sums_ref)

    codes = codes_ref[...].reshape(group * padded, codes_ref.shape[2])
    second_grad = gather_rows(codes, returned)
    unit, inverse = normal(attended_ref[...].reshape(group * padded, width))
    sums_ref[2:3, :] += jnp.sum(second_grad * unit, 0, keepdims=True)
    sums_ref[3:4, :] += jnp.sum(second_grad, 0, keepdims=True)
    attended_grad = padded_rows(cotangent_ref, buffer) + norm_back(
        second_grad, vector_ref[2:3, :], unit, inverse
    )
    buffer[...] = attended_grad
    branch = attended_grad.astype(BF16)
    branch_ref[...] = branch.reshape(group, padded, width)
    mixed_grad_ref[...] = (
        dot(branch, out_weight_ref[...], NT).astype(BF16).reshape(group, padded, width)
    )
    scale = (width // HEADS) ** (-0.5)
    heads = LANES * HEADS // width
    lane = lax.broadcasted_iota(jnp.int32, (padded, LANES), 1) // (width // HEADS)
    real = lax.broadcasted_iota(jnp.int32, (padded, heads * padded), 0) < length
    for image in range(group):
        for at in range(0, width, LANES):
            query = qkv_ref[image, :, at : at + LANES].astype(F32) * scale
            keys = qkv_ref[image, :, width + at : width + at + LANES]
            values = qkv_ref[image, :, 2 * width + at : 2 * width + at + LANES]
            result = mixed_grad_ref[image, :, at : at + LANES].astype(F32)
            queries = stacked(query, lane, heads)
            results = stacked(result, lane, heads)
            scores = jnp.where(real, dot(keys, queries, NT), -1e30)
            prob_grad = dot(values, results, NT)
            raised = jnp.exp(scores - jnp.max(scores, 0, keepdims=True))
            probs = raised * (1.0 / jnp.sum(raised, 0, keepdims=True))
            score_grad = (
                probs * (prob_grad - jnp.sum(probs * prob_grad, 0, keepdims=True))
            ).astype(BF16)
            keys_scaled = (keys.astype(F32) * scale).astype(BF16)
            grads = (
                unstacked(dot(score_grad, keys_scaled, TN), lane, heads),
                dot(score_grad, queries),
                dot(probs.astype(BF16), results),
            )
            for index, grad in enumerate(grads):
                start = index * width + at
                rows_grad_ref[image, :, start : start + LANES] = grad.astype(BF16)
    rows_grad = rows_grad_ref[...].reshape(group * padded, 3 * width)
    first_grad = dot(rows_grad, qkv_weight_ref[...], NT)
    attended_grad = buffer[...]
    unit, inverse = normal(padded_rows(tokens_ref, buffer))
    sums_ref[0:1, :] += jnp.sum(first_grad * unit, 0, keepdims=True)
    sums_ref[1:2, :] += jnp.sum(first_grad, 0, keepdims=True)
    tokens_grad = attended_grad + norm_back(first_grad, vector_ref[0:1, :], unit, inverse)
    for image in range(group):
        tokens_grad_ref[image] = tokens_grad[
            image * padded : image * padded + length, :
        ].astype(BF16)


def attend_back(codes, returned, cotangent, tokens, attended, qkv, weights, vectors):
    images, length, width = tokens.shape
    padded = attended.shape[1]
    group = group_of(images)
    rows = images * padded
    image = lambda count, cols: pl.BlockSpec((group, count, cols), lambda i: (i, 0, 0))
    return call(
        attend_back_kernel,
        (images // group,),
        [image(padded, codes.shape[2])]
        + [whole(array.shape) for array in returned]
        + [
            image(length, width), image(length, width), image(padded, width), image(padded, 3 * width),
            pl.BlockSpec((width, 3 * width), lambda i: (0, 0), pipeline_mode=pl.Buffered(1)),
            pl.BlockSpec((width, width), lambda i: (0, 3), pipeline_mode=pl.Buffered(1)),
            whole(vectors.shape),
        ],
        [image(length, width), image(padded, width), image(padded, 3 * width), whole((8, width))],
        [
            jax.ShapeDtypeStruct((images, length, width), BF16),
            jax.ShapeDtypeStruct((images, padded, width), BF16),
            jax.ShapeDtypeStruct((images, padded, 3 * width), BF16),
            jax.ShapeDtypeStruct((8, width), F32),
        ],
        [pltpu.VMEM((group * padded, width), F32), pltpu.VMEM((group, padded, width), BF16)],
        56,
        cost(
            rows * width * (4 * width + 10 * padded + CHUNKS * returned[0].shape[0]),
            rows * width * 24 + width * (width * 8 + 4 * returned[0].shape[0]),
            rows * padded * HEADS,
        ),
    )(codes, *returned, cotangent, tokens, attended, qkv, weights, weights, vectors)


def combine_kernel(codes_ref, *refs):
    *returned, attended_ref, out_ref = refs
    group, padded, width = attended_ref.shape
    codes = codes_ref[...].reshape(group * padded, codes_ref.shape[2])
    total = attended_ref[...].reshape(group * padded, width) + gather_rows(codes, returned)
    for image in range(group):
        at = image * padded
        out_ref[image] = total[at : at + out_ref.shape[1], :].astype(BF16)


def combine(codes, returned, attended, length):
    images, padded, width = attended.shape
    group = group_of(images)
    image = lambda rows, cols: pl.BlockSpec((group, rows, cols), lambda i: (i, 0, 0))
    return call(
        combine_kernel,
        (images // group,),
        [image(padded, codes.shape[2])]
        + [whole(array.shape) for array in returned]
        + [image(padded, width)],
        image(length, width),
        jax.ShapeDtypeStruct((images, length, width), BF16),
        [],
        40,
        cost(
            images * padded * width * sum(array.shape[0] for array in returned),
            images * padded * width * 8,
        ),
    )(codes, *returned, attended)


def sum_shards(array):
    size = lax.axis_size("shard")
    rows, cols = array.shape
    pairs = size // 2
    me = lax.axis_index("shard")
    blocks = array.reshape(pairs, 2, rows // size, cols)
    take = lambda core: lax.dynamic_index_in_dim(blocks, core, 1, keepdims=False)
    other = lax.ppermute(take(1 - me % 2), "shard", [(s, s ^ 1) for s in range(size)])
    halves = take(me % 2).astype(F32) + other.astype(F32)
    sent = halves.astype(BF16)
    at = me // 2
    total = lax.dynamic_index_in_dim(halves, at, 0, keepdims=False)
    for shift in range(1, pairs):
        part = lax.dynamic_index_in_dim(sent, (at + shift) % pairs, 0, keepdims=False)
        moves = [(s, (s // 2 + shift) % pairs * 2 + s % 2) for s in range(size)]
        total = total + lax.ppermute(part, "shard", moves).astype(F32)
    return total.astype(BF16)


def sum_experts(array):
    experts = lax.axis_size("expert")
    rows, cols = array.shape
    parts = exchange(array.reshape(experts, rows // experts, cols))
    share = jnp.sum(parts.astype(F32), 0).astype(BF16)
    shares = exchange(jnp.broadcast_to(share[None], parts.shape))
    return shares.reshape(rows, cols).astype(F32)


def exchange(array):
    return lax.all_to_all(array, "expert", split_axis=0, concat_axis=0, tiled=True)


def shards(
    tokens,
    ln1_gain,
    ln1_bias,
    qkv_weight,
    out_weight,
    ln2_gain,
    ln2_bias,
    router_weight,
    up_weight,
    down_weight,
    routes,
    slots,
    keep,
    cotangent,
):
    images, length, width = tokens.shape
    rows = images * length
    experts = lax.axis_size("expert")
    assert up_weight.shape[1] == 1 and router_weight.shape[1] == experts
    capacity = max(4, 5 * rows // (2 * experts))
    count = -(-capacity // (16 * CHUNKS)) * 16
    padded = -(-length // 16) * 16

    routes, slots, keep = (array.transpose(0, 2, 1) for array in (routes, slots, keep))
    fill = ((0, 0), (0, 0), (0, padded - length))
    flat_codes = lambda codes: (
        jnp.pad(codes, fill, constant_values=-1).transpose(1, 0, 2).reshape(2, images * padded)
    )
    all_codes = jnp.where(keep > 0, routes * (CHUNKS * count) + slots, -1)
    g_sent = send(cotangent, flat_codes(all_codes), experts, CHUNKS * count, width)
    g_sent, tokens_in, qkv_weight, routes, slots, keep = lax.optimization_barrier(
        (g_sent, tokens, qkv_weight, routes, slots, keep)
    )
    g_here = exchange(g_sent)

    columns = experts + 4
    spare = -columns % LANES
    small = jnp.concatenate(
        [router_weight, jnp.stack([ln1_gain, ln1_bias, ln2_gain, ln2_bias], 1)], 1
    )
    packed = jnp.concatenate(
        [qkv_weight, out_weight, jnp.pad(small, ((0, 0), (0, spare)))], 1
    )
    weights = lax.all_gather(packed, "shard", axis=0, tiled=True)
    vectors = jnp.pad(
        weights[:, 4 * width + experts : 4 * width + columns].T.astype(F32), ((0, 4), (0, 0))
    )

    chunk_codes = []
    for chunk in range(CHUNKS):
        place = slots - chunk * count
        here = (keep > 0) & (place >= 0) & (place < count)
        chunk_codes.append(jnp.where(here, routes * count + place, -1))
    row_codes = [flat_codes(codes) for codes in chunk_codes]
    codes = jnp.pad(
        jnp.concatenate(chunk_codes, 1), fill, constant_values=-1
    ).transpose(0, 2, 1)

    up = lax.all_gather(up_weight.reshape(-1, width), "shard", axis=0, tiled=True)
    down = lax.all_gather(down_weight.reshape(-1, width), "shard", axis=0, tiled=True)

    qkv, mixed, attended, first, second = attend(tokens_in, weights, vectors, padded)
    flat_second = second.reshape(images * padded, width)
    mine = (
        lax.broadcasted_iota(jnp.int32, (8, LANES), 1) == lax.axis_index("expert")
    ).astype(F32)

    back_here, out_here, wide, up_parts = [], [], [], []
    for chunk in range(CHUNKS):
        x = exchange(send(flat_second, row_codes[chunk], experts, count, width))
        if chunk:
            x, up_parts = lax.optimization_barrier((x, up_parts))
        out, *made, back = run_expert(chunk, mine, x, g_here, up, down, weights, experts)
        out_here.append(out)
        back_here.append(back)
        wide.append((*made, x.reshape(experts * count, width)))
        if chunk < CHUNKS - 1:
            up_parts.append(dot(made[1], wide[chunk][4], TN))
    returned = []
    for chunk in range(CHUNKS):
        back = back_here[chunk]
        if chunk:
            back, wide, returned = lax.optimization_barrier((back, wide, returned))
        returned.append(exchange(back).reshape(experts * count, width))

    down_full = sum(dot(active, scaled, TN) for active, _, scaled, _, _ in wide).astype(BF16)
    _, before, _, _, x = wide[-1]
    up_full = sum(up_parts, dot(before, x, TN)).astype(BF16)
    router_full = sum(dot(x, logit, TN) for _, _, _, logit, x in wide)
    down_full, up_full, router_full, returned = lax.optimization_barrier(
        (down_full, up_full, router_full, returned)
    )
    out_returned = []
    for out in out_here:
        out, _, _ = lax.optimization_barrier((out, returned, out_returned))
        out_returned.append(exchange(out).reshape(experts * count, width))
    down_grad = lax.psum_scatter(down_full, "shard", scatter_dimension=0, tiled=True)

    tokens_grad, branch, rows_grad, sums = attend_back(
        codes, returned, cotangent, tokens, attended, qkv, weights, vectors
    )
    flat = lambda array: array.reshape(images * padded, -1)
    qkv_full = dot(flat(first), flat(rows_grad), TN)
    out_full = dot(flat(mixed), flat(branch), TN)
    small_full = jnp.concatenate([router_full[:, :experts], sums[0:4].T], 1)
    layer = jnp.concatenate(
        [qkv_full, out_full, jnp.pad(small_full, ((0, 0), (0, spare)))], 1
    ).astype(BF16)
    layer, out_returned[0] = lax.optimization_barrier((layer, out_returned[0]))
    layer = sum_shards(layer)
    layer, up_full = lax.optimization_barrier((layer, up_full))
    up_grad = lax.psum_scatter(up_full, "shard", scatter_dimension=0, tiled=True)
    layer, out_returned = lax.optimization_barrier((layer, out_returned))
    layer = sum_experts(layer)
    block_out = combine(codes, out_returned, attended, length)
    tail = 4 * width + experts
    return (
        block_out,
        tokens_grad,
        layer[:, tail],
        layer[:, tail + 1],
        layer[:, : 3 * width],
        layer[:, 3 * width : 4 * width],
        layer[:, tail + 2],
        layer[:, tail + 3],
        layer[:, 4 * width : tail],
        up_grad.astype(F32)[:, None, :],
        down_grad.astype(F32)[:, None, :],
    )


def solution(mesh):
    placed = (
        P(("expert", "shard"), None, None),
        P("shard"),
        P("shard"),
        P("shard", None),
        P("shard", None),
        P("shard"),
        P("shard"),
        P("shard", None),
        P("shard", "expert", None),
        P("shard", "expert", None),
        P(("expert", "shard"), None, None),
        P(("expert", "shard"), None, None),
        P(("expert", "shard"), None, None),
        P(("expert", "shard"), None, None),
    )
    return jax.shard_map(
        shards,
        mesh=mesh,
        in_specs=placed,
        out_specs=(
            P(("expert", "shard"), None, None),
            P(("expert", "shard"), None, None),
            P("shard"),
            P("shard"),
            P("shard", None),
            P("shard", None),
            P("shard"),
            P("shard"),
            P("shard", None),
            P("shard", "expert", None),
            P("shard", "expert", None),
        ),
        check_vma=False,
    )
```
